128 devices in a mesh: dom: 128 (over y, z, x, core).
Axes of the slice: x: 4, y: 4, z: 4, core: 2. Of those that a mesh axis runs over, the one named last changes fastest.
Arguments:
- thickness: float32 [16, 262144], P(None, 'dom'), may hold values from 0.5 to 1.5
- velocity: float32 [16, 786432], P(None, 'dom'), may hold values from -4 to 4
- send_cells: int32 [512, 256], P('dom'), may hold values from 0 to 2047
- send_edges: int32 [512, 512], P('dom'), may hold values from 0 to 6143
- cell_edges: int32 [6, 262144], P(None, 'dom'), may hold values from 0 to 8191
- cell_orient: int32 [6, 262144], P(None, 'dom'), may hold values from 0 to 1
- edge_cells: int32 [2, 786432], P(None, 'dom'), may hold values from 0 to 3071
- edge_edges: int32 [10, 786432], P(None, 'dom'), may hold values from 0 to 8191
- edge_weights: float32 [10, 786432], P(None, 'dom'), may hold values from -2 to 2
- cell_area: float32 [262144], P('dom'), may hold values from 2 to 6
- edge_spacing: float32 [786432], P('dom'), may hold values from 0.5 to 2
- edge_length: float32 [786432], P('dom'), may hold values from 0.5 to 2
- coriolis: float32 [786432], P('dom'), may hold values from 0.5 to 1.5
Outputs:
- new_thickness: float32 [16, 262144], P(None, 'dom')
- new_velocity: float32 [16, 786432], P(None, 'dom')
The draws below stay inside these ranges and needn't reach their ends.
Inputs may be any that keep to these rules, and one draw needn't show every extreme that they name: `cell_edges`: extended local edge numbers, owned edges first, then halo slots in order of j. `edge_cells`: extended local cell numbers, owned cells first, then halo slots in order of j.
All inputs are finite; a program needn't handle non-finite values.
Results may differ from the reference program's by a relative error of at most 0.0001.
Values sent between devices are 32-bit elements; how exact they have to be, the bound alone decides.
A program may use at most 128 MiB of HBM per device.

```python
import math
import jax
import jax.numpy as jnp
from jax import lax

LEVELS = 16
CELLS_DEV = 2048
EDGES_DEV = 6144
SIDES = 6
NEIGHBOURS = 10
REACH = 2
SLOT = 256
EDGE_SLOT = 512
CELLS = 262144
EDGES = 786432
N_DOM = 128


def touch_ends(values, rng, least, high):
    shape = values.shape
    index_at = [jax.random.randint(jax.random.fold_in(rng, axis), (), 0, shape[axis]) for axis in range(len(shape))]
    values = values.at[tuple(index_at)].set(least)
    longest = shape.index(max(shape))
    index_at[longest] = (index_at[longest] + 1) % shape[longest]
    return values.at[tuple(index_at)].set(high)


def block_levels(own_key, shape, cuts, low, high):
    gain = 1.0
    for axis_at, parts in cuts:
        heights = jax.random.uniform(jax.random.fold_in(jax.random.fold_in(own_key, 6), axis_at), (parts,), jnp.float32, low / len(cuts), high / len(cuts))
        gain = gain * jnp.repeat(jnp.exp(heights), shape[axis_at] // parts).reshape((-1,) + (1,) * (len(shape) - 1 - axis_at))
    return gain


def bell_draw(own_key, shape, width, reach, shards=(), held_as=jnp.bfloat16):
    entries = jax.random.normal(own_key, shape, jnp.float32) * width
    if len(shards) > 0:
        entries = block_levels(own_key, shape, shards, -0.22, 0.18) * entries
    return jnp.clip(entries, min=-reach, max=reach).astype(held_as)


def setup_inputs(seed: int = 0) -> dict:
    seeds = jax.random.split(jax.random.key(seed), 14)
    thickness = jnp.clip(0.5 + 1.0 * jax.random.uniform(seeds[0], (LEVELS, CELLS), jnp.float32) ** block_levels(seeds[0], (LEVELS, CELLS), ((1, 128),), -0.2, 0.2), 0.5, 1.5)
    velocity = bell_draw(seeds[1], (LEVELS, EDGES), 1.0, 4.0, ((1, 128),), jnp.float32)
    send_cells = touch_ends(jax.random.randint(seeds[2], (N_DOM * 2 * REACH, SLOT), 0, CELLS_DEV), jax.random.fold_in(seeds[2], 1), 0, CELLS_DEV - 1).astype(jnp.int32)
    send_edges = touch_ends(jax.random.randint(seeds[3], (N_DOM * 2 * REACH, EDGE_SLOT), 0, EDGES_DEV), jax.random.fold_in(seeds[3], 1), 0, EDGES_DEV - 1).astype(jnp.int32)
    cell_edges = touch_ends(jax.random.randint(seeds[4], (SIDES, CELLS), 0, EDGES_DEV + 2 * REACH * EDGE_SLOT), jax.random.fold_in(seeds[4], 1), 0, (EDGES_DEV + 2 * REACH * EDGE_SLOT) - 1).astype(jnp.int32)
    cell_orient = touch_ends(jax.random.randint(seeds[5], (SIDES, CELLS), 0, 2), jax.random.fold_in(seeds[5], 1), 0, 1).astype(jnp.int32)
    edge_cells = touch_ends(jax.random.randint(seeds[6], (2, EDGES), 0, CELLS_DEV + 2 * REACH * SLOT), jax.random.fold_in(seeds[6], 1), 0, (CELLS_DEV + 2 * REACH * SLOT) - 1).astype(jnp.int32)
    edge_edges = touch_ends(jax.random.randint(seeds[7], (NEIGHBOURS, EDGES), 0, EDGES_DEV + 2 * REACH * EDGE_SLOT), jax.random.fold_in(seeds[7], 1), 0, (EDGES_DEV + 2 * REACH * EDGE_SLOT) - 1).astype(jnp.int32)
    edge_weights = bell_draw(seeds[8], (NEIGHBOURS, EDGES), NEIGHBOURS ** -0.5, 2.0, ((1, 128),), jnp.float32)
    cell_area = jnp.clip(jnp.exp(math.log(6.0) - 1.0986123 * jax.random.uniform(seeds[9], (CELLS,), jnp.float32) ** block_levels(seeds[9], (CELLS,), ((0, 128),), -0.2, 0.2)), 2.0, 6.0)
    edge_spacing = jnp.clip(jnp.exp(math.log(2.0) - 1.3862944 * jax.random.uniform(seeds[10], (EDGES,), jnp.float32) ** block_levels(seeds[10], (EDGES,), ((0, 128),), -0.2, 0.2)), 0.5, 2.0)
    edge_length = jnp.clip(jnp.exp(math.log(2.0) - 1.3862944 * jax.random.uniform(seeds[11], (EDGES,), jnp.float32) ** block_levels(seeds[11], (EDGES,), ((0, 128),), -0.2, 0.2)), 0.5, 2.0)
    coriolis = jnp.clip(0.5 + 1.0 * jax.random.uniform(seeds[12], (EDGES,), jnp.float32) ** block_levels(seeds[12], (EDGES,), ((0, 128),), -0.2, 0.2), 0.5, 1.5)
    return dict(thickness=thickness, velocity=velocity, send_cells=send_cells, send_edges=send_edges, cell_edges=cell_edges, cell_orient=cell_orient, edge_cells=edge_cells, edge_edges=edge_edges, edge_weights=edge_weights, cell_area=cell_area, edge_spacing=edge_spacing, edge_length=edge_length, coriolis=coriolis)


gravity = 0.1
mixing = 0.2
time_step = 0.5


def to_parts(array):
    if array.ndim == 1:
        return array.reshape(N_DOM, -1)
    return array.reshape(array.shape[0], N_DOM, -1).transpose(1, 0, 2)


def from_parts(array):
    return array.transpose(1, 0, 2).reshape(array.shape[1], -1)


def deliver(blocks):
    slots = blocks.shape[1]
    half = slots // 2
    pieces = []
    for place in range(slots):
        offset = place - half if place < half else place - half + 1
        column = blocks[:, place]
        empty = jnp.zeros_like(column[:abs(offset)])
        if offset > 0:
            moved = jnp.concatenate([empty, column[:N_DOM - offset]], axis=0)
        else:
            moved = jnp.concatenate([column[-offset:], empty], axis=0)
        pieces.append(moved)
    return jnp.concatenate(pieces, axis=2)


def collect(fields, lists):
    blocks = jax.vmap(lambda field, rows: jnp.take(field, rows, axis=1))(fields, lists)
    return deliver(blocks.transpose(0, 2, 1, 3))


def column_pressure(height):
    return gravity * (jnp.cumsum(height, axis=0) - 0.5 * height)


def edge_section(items):
    (velocity, state_h, state_u, halo_h, halo_u, edge_cells, edge_edges,
     edge_weights, edge_spacing, edge_length, coriolis, step_size) = items
    ext_h = jnp.concatenate([state_h, halo_h], axis=1)
    ext_u = jnp.concatenate([state_u, halo_u], axis=1)
    left_h = jnp.take(ext_h, edge_cells[0], axis=1)
    right_h = jnp.take(ext_h, edge_cells[1], axis=1)
    gradient = (column_pressure(right_h) - column_pressure(left_h)) / edge_spacing
    beside_all = jnp.take(ext_u, edge_edges, axis=1)
    tangent = jnp.sum(beside_all * edge_weights[None], axis=1)
    upper = jnp.concatenate([state_u[:1], state_u[:-1]], axis=0)
    lower = jnp.concatenate([state_u[1:], state_u[-1:]], axis=0)
    blend = mixing * (upper + lower - 2.0 * state_u)
    u_next = velocity + step_size * (-gradient + coriolis * tangent + blend)
    flux = u_next * 0.5 * (left_h + right_h) * edge_length
    return u_next, flux


def cell_section(items):
    thickness, flux, halo_f, cell_edges, cell_orient, cell_area, step_size = items
    ext_f = jnp.concatenate([flux, halo_f], axis=1)
    signs = (2 * cell_orient - 1).astype(jnp.float32)
    spread = jnp.sum(jnp.take(ext_f, cell_edges, axis=1) * signs[None], axis=1)
    return thickness - step_size * spread / cell_area


def reference(thickness, velocity, send_cells, send_edges, cell_edges, cell_orient, edge_cells, edge_edges, edge_weights, cell_area, edge_spacing, edge_length, coriolis):
    thick_p = to_parts(thickness)
    veloc_p = to_parts(velocity)
    send_c = send_cells.reshape(N_DOM, -1, send_cells.shape[1])
    send_e = send_edges.reshape(N_DOM, -1, send_edges.shape[1])
    cedges = to_parts(cell_edges)
    corient = to_parts(cell_orient)
    ecells = to_parts(edge_cells)
    eedges = to_parts(edge_edges)
    eweights = to_parts(edge_weights)
    area_p = to_parts(cell_area)
    spacing_p = to_parts(edge_spacing)
    length_p = to_parts(edge_length)
    cori_p = to_parts(coriolis)
    state_h = thick_p
    state_u = veloc_p
    for section in range(3):
        step_size = jnp.full((N_DOM,), time_step / (3 - section), jnp.float32)
        halo_h = collect(state_h, send_c)
        halo_u = collect(state_u, send_e)
        u_next, flux = lax.map(edge_section, (veloc_p, state_h, state_u, halo_h, halo_u, ecells, eedges, eweights, spacing_p, length_p, cori_p, step_size))
        halo_f = collect(flux, send_e)
        state_h = lax.map(cell_section, (thick_p, flux, halo_f, cedges, corient, area_p, step_size))
        state_u = u_next
    return from_parts(state_h), from_parts(state_u)
```

```python
import functools

import jax
import jax.numpy as jnp
from jax import lax
from jax.experimental import pallas as pl
from jax.experimental.pallas import tpu as pltpu
from jax.sharding import PartitionSpec as P

gravity = 0.1
mixing = 0.2
time_step = 0.5
LANES = 128
BLOCK = 32
STEP = 8
OFFSETS = (-2, -1, 1, 2)
VMEM = pltpu.VMEM
SMEM = pltpu.SMEM


class Plan:
    def __init__(self, terms, octets, chunks, cap, weighted):
        self.terms, self.octets, self.chunks, self.cap, self.weighted = terms, octets, chunks, cap, weighted

    def shapes(self):
        blocks = self.octets * self.cap // BLOCK
        raw = (self.terms, self.octets * 8, LANES)
        out = [
            jax.ShapeDtypeStruct(raw, jnp.int32),
            jax.ShapeDtypeStruct((self.octets * self.cap, LANES), jnp.int32),
            jax.ShapeDtypeStruct((-(-blocks // 8) * 8, LANES), jnp.int32),
            jax.ShapeDtypeStruct((self.octets,), jnp.int32),
        ]
        if self.weighted:
            out += [
                jax.ShapeDtypeStruct(raw, jnp.float32),
                jax.ShapeDtypeStruct((self.octets * self.cap, LANES), jnp.float32),
            ]
        return out

    def out_specs(self):
        spaces = [VMEM, VMEM, VMEM, SMEM] + [VMEM, VMEM] * self.weighted
        return [pl.BlockSpec(memory_space=s) for s in spaces]

    def in_specs(self):
        spaces = [VMEM, VMEM, SMEM, SMEM] + [VMEM, VMEM] * self.weighted
        return [pl.BlockSpec(memory_space=s) for s in spaces]

    def count(self):
        return 6 if self.weighted else 4


AROUND = Plan(10, 6, 64, 384, True)
PAIR = Plan(1, 12, 24, 96, False)
SIDE = Plan(6, 2, 64, 320, True)
SEND_E = Plan(1, 2, 48, 128, False)
SEND_C = Plan(1, 1, 16, 64, False)


def iota(axis):
    return lax.broadcasted_iota(jnp.int32, (8, LANES), axis)


def spread_row(ref, *at):
    return jnp.broadcast_to(ref[at], (8, LANES))


def build(plan, refs, keys, loads):
    raw, packed, chunk_of, counts = refs[:4]
    sub, lane = iota(0), iota(1)

    def octet(o, carry):
        at = pl.ds(pl.multiple_of(o * 8, 8), 8)
        chunk = [lax.shift_right_logical(raw[k, at, :], 7) for k in range(plan.terms)]
        base = jnp.zeros((8, LANES), jnp.int32)
        key = [jnp.zeros((8, LANES), jnp.int32) for _ in range(plan.terms)]
        for c in range(plan.chunks):
            hit = [chunk[k] == c for k in range(plan.terms)]
            one = [h.astype(jnp.int32) for h in hit]
            total = one[0]
            for k in range(1, plan.terms):
                total = total + one[k]
            upto = total
            for shift in (1, 2, 4):
                upto = upto + jnp.where(sub >= shift, pltpu.roll(upto, shift, 0), 0)
            rounds = jnp.max(jnp.max(upto, axis=1, keepdims=True), axis=0, keepdims=True)
            start = base + upto - total
            for k in range(plan.terms):
                key[k] = jnp.where(hit[k], start, key[k])
                if k + 1 < plan.terms:
                    start = start + one[k]
            base = base + rounds
        number = base[0, 0]
        counts[o] = number
        for k in range(plan.terms):
            keys[k] = key[k]
            loads[k] = (raw[k, at, :] & 127) | (sub << 7) | (chunk[k] << 11)

        def block(b, carry):
            row = [sub + (b * BLOCK + 8 * v) for v in range(BLOCK // 8)]
            load = [jnp.full((8, LANES), 8 << 7, jnp.int32) for _ in row]
            weight = [jnp.zeros((8, LANES), jnp.float32) for _ in row]
            for k in range(plan.terms):
                for s in range(8):
                    wanted = spread_row(keys, k, pl.ds(s, 1), slice(None))
                    value = spread_row(loads, k, pl.ds(s, 1), slice(None))
                    if plan.weighted:
                        scale = spread_row(refs[4], k, pl.ds(o * 8 + s, 1), slice(None))
                    for v in range(BLOCK // 8):
                        here = wanted == row[v]
                        load[v] = jnp.where(here, value, load[v])
                        if plan.weighted:
                            weight[v] = jnp.where(here, scale, weight[v])
            ids = jnp.zeros((8, LANES), jnp.int32)
            for v in range(BLOCK // 8):
                to = pl.ds(pl.multiple_of(o * plan.cap + b * BLOCK + 8 * v, 8), 8)
                packed[to, :] = load[v] & 2047
                if plan.weighted:
                    refs[5][to, :] = weight[v]
                own = jnp.max(load[v] >> 11, axis=1, keepdims=True)
                ids = ids + jnp.where(lane == sub + 8 * v, own, 0)
            chunk_of[pl.ds(o * (plan.cap // BLOCK) + b, 1), :] = jnp.sum(ids, axis=0, keepdims=True)
            return carry

        lax.fori_loop(0, (jnp.minimum(number, plan.cap) + BLOCK - 1) // BLOCK, block, 0)
        return carry

    lax.fori_loop(0, plan.octets, octet, 0)


def lanes_at(position):
    return pl.ds(pl.multiple_of(position * LANES, LANES), LANES)


def gather(plan, refs, o, sources, put, add):
    raw, packed, chunk_of, counts = refs[:4]
    number = counts[o]
    total = 8 * len(sources)
    empty = tuple(jnp.zeros((8, LANES), jnp.float32) for _ in range(total))

    def finish(sums):
        for d in range(8):
            for i in range(len(sources)):
                put(d, i, sums[d * len(sources) + i])

    @pl.when(number <= plan.cap)
    def _():
        def step(t, sums):
            sums = list(sums)
            for r in range(STEP):
                row = t * STEP + r
                c = chunk_of[o * (plan.cap // BLOCK) + row // BLOCK, row % BLOCK]
                at = o * plan.cap + row
                load = spread_row(packed, pl.ds(at, 1), slice(None))
                pick, goal = load & 127, lax.shift_right_logical(load, 7)
                if plan.weighted:
                    scale = spread_row(refs[5], pl.ds(at, 1), slice(None))
                values = []
                for ref, rows in sources:
                    value = jnp.take_along_axis(ref[rows, lanes_at(c)], pick, axis=1, mode="promise_in_bounds")
                    values.append(value * scale if plan.weighted else value)
                for d in range(8):
                    mine = goal == d
                    for i, value in enumerate(values):
                        j = d * len(sources) + i
                        sums[j] = sums[j] + jnp.where(mine, value, 0.0) if add else jnp.where(mine, value, sums[j])
            return tuple(sums)

        finish(lax.fori_loop(0, (number + STEP - 1) // STEP, step, empty))

    @pl.when(number > plan.cap)
    def _():
        for d in range(8):
            sums = tuple(jnp.zeros((8, LANES), jnp.float32) for _ in sources)
            for k in range(plan.terms):
                index = spread_row(raw, k, pl.ds(o * 8 + d, 1), slice(None))
                pick, chunk = index & 127, lax.shift_right_logical(index, 7)

                def look(c, found):
                    out = []
                    for (ref, rows), old in zip(sources, found):
                        value = jnp.take_along_axis(ref[rows, lanes_at(c)], pick, axis=1, mode="promise_in_bounds")
                        out.append(jnp.where(chunk == c, value, old))
                    return tuple(out)

                found = lax.fori_loop(0, plan.chunks, look, tuple(jnp.zeros((8, LANES), jnp.float32) for _ in sources))
                if plan.weighted:
                    scale = spread_row(refs[4], k, pl.ds(o * 8 + d, 1), slice(None))
                    found = tuple(f * scale for f in found)
                sums = tuple(s + f for s, f in zip(sums, found))
            for i in range(len(sources)):
                put(d, i, sums[i])


TOP, LOW = slice(0, 8), slice(8, 16)


def both(*refs):
    return [(ref, rows) for ref in refs for rows in (TOP, LOW)]


def sends_kernel(h, u, send_c, send_e, *rest):
    plan_e, plan_c, (out, keys, loads, ids_e, ids_c) = rest[:4], rest[4:8], rest[8:]
    for j in range(4):
        for q in range(4):
            plan_e[0][0, 4 * j + q : 4 * j + q + 1, :] = send_e[j : j + 1, q * LANES : (q + 1) * LANES]
        for q in range(2):
            plan_c[0][0, 2 * j + q : 2 * j + q + 1, :] = send_c[j : j + 1, q * LANES : (q + 1) * LANES]
    build(SEND_E, plan_e, keys, loads)
    build(SEND_C, plan_c, keys, loads)
    pltpu.sync_copy(plan_e[2], ids_e)
    pltpu.sync_copy(plan_c[2], ids_c)
    plan_e = (*plan_e[:2], ids_e, plan_e[3])
    plan_c = (*plan_c[:2], ids_c, plan_c[3])
    for o in range(2):

        def put_u(d, i, value):
            j, q = (o * 8 + d) // 4, (o * 8 + d) % 4
            out[8 * i : 8 * i + 8, j * 768 + q * LANES : j * 768 + (q + 1) * LANES] = value

        gather(SEND_E, plan_e, o, both(u), put_u, False)

    def put_h(d, i, value):
        j, q = d // 2, d % 2
        out[8 * i : 8 * i + 8, j * 768 + 512 + q * LANES : j * 768 + 512 + (q + 1) * LANES] = value

    gather(SEND_C, plan_c, 0, both(h), put_h, False)


def plans_kernel(edge_edges, edge_weights, edge_cells, cell_edges, cell_orient, *rest):
    around, pair, side = rest[:6], rest[6:10], rest[10:16]
    keys, loads = rest[16:]
    for g in range(48):
        at = slice(g * LANES, (g + 1) * LANES)
        for k in range(10):
            around[0][k, g : g + 1, :] = edge_edges[k : k + 1, at]
            around[4][k, g : g + 1, :] = edge_weights[k : k + 1, at]
        for k in range(2):
            to = g // 4 * 8 + k * 4 + g % 4
            pair[0][0, to : to + 1, :] = edge_cells[k : k + 1, at]
    for g in range(16):
        at = slice(g * LANES, (g + 1) * LANES)
        for k in range(6):
            side[0][k, g : g + 1, :] = cell_edges[k : k + 1, at]
            side[4][k, g : g + 1, :] = (2 * cell_orient[k : k + 1, at] - 1).astype(jnp.float32)
    build(AROUND, around, keys, loads)
    build(PAIR, pair, keys, loads)
    build(SIDE, side, keys, loads)


def below(x, shift):
    return pltpu.roll(x, shift, 0)


def edge_kernel(tau, last, u_place, h_place, *refs):
    velocity, u_own, h_own, halo_u, halo_h, spacing, length, coriolis = refs[:8]
    around, pair, refs = refs[8:14], refs[14:18], refs[18:]
    send_e, (u_next, flux, out, ext_u, ext_h, tangent, cells) = refs[:4], refs[4:]
    ext_u[:, : 48 * LANES] = u_own[...]
    ext_h[:, : 16 * LANES] = h_own[...]
    for j in range(4):
        at = j * u_place[0] + u_place[1]
        ext_u[:, 48 * LANES + 512 * j : 48 * LANES + 512 * (j + 1)] = halo_u[:, at : at + 512]
        at = j * h_place[0] + h_place[1]
        ext_h[:, 16 * LANES + 256 * j : 16 * LANES + 256 * (j + 1)] = halo_h[:, at : at + 256]
    sub = iota(0)

    def running(x):
        for shift in (1, 2, 4):
            x = x + jnp.where(sub >= shift, below(x, shift), 0.0)
        return x

    def octet(o, carry):
        def put_tangent(d, i, value):
            tangent[8 * i : 8 * i + 8, d * LANES : (d + 1) * LANES] = value

        gather(AROUND, around, o, both(ext_u), put_tangent, True)
        for half in range(2):

            def put_cells(d, i, value):
                cells[8 * i : 8 * i + 8, d * LANES : (d + 1) * LANES] = value

            gather(PAIR, pair, o * 2 + half, both(ext_h), put_cells, False)
            for q in range(4):
                group = o * 8 + half * 4 + q
                at = lanes_at(group)
                left, right = slice(q * LANES, (q + 1) * LANES), slice((q + 4) * LANES, (q + 5) * LANES)
                step = [cells[rows, right] - cells[rows, left] for rows in (TOP, LOW)]
                mean = [0.5 * (cells[rows, right] + cells[rows, left]) for rows in (TOP, LOW)]
                column = [running(x) for x in step]
                column[1] = column[1] + jnp.broadcast_to(column[0][7:8], (8, LANES))
                pressure = [gravity * (c - 0.5 * x) for c, x in zip(column, step)]
                u = [u_own[rows, at] for rows in (TOP, LOW)]
                upper = [
                    jnp.where(sub == 0, u[0], below(u[0], 1)),
                    jnp.where(sub == 0, jnp.broadcast_to(u[0][7:8], (8, LANES)), below(u[1], 1)),
                ]
                lower = [
                    jnp.where(sub == 7, jnp.broadcast_to(u[1][0:1], (8, LANES)), below(u[0], 7)),
                    jnp.where(sub == 7, u[1], below(u[1], 7)),
                ]
                own = [spread_row(ref, pl.ds(group, 1), slice(None)) for ref in (spacing, length, coriolis)]
                here = slice((half * 4 + q) * LANES, (half * 4 + q + 1) * LANES)
                for i, rows in enumerate((TOP, LOW)):
                    mix = mixing * (upper[i] + lower[i] - 2.0 * u[i])
                    slope = -pressure[i] / own[0] + own[2] * tangent[rows, here] + mix
                    fresh = velocity[rows, at] + tau * slope
                    u_next[rows, at] = fresh
                    flux[rows, at] = fresh * mean[i] * own[1]
        return carry

    lax.fori_loop(0, 6, octet, 0)
    sources = both(flux) if last else both(flux, u_next)
    width = 512 if last else 1024
    for o in range(2):

        def put_send(d, i, value):
            j, q = (o * 8 + d) // 4, (o * 8 + d) % 4
            at = j * width + (i // 2) * 512 + q * LANES
            out[8 * (i % 2) : 8 * (i % 2) + 8, at : at + LANES] = value

        gather(SEND_E, send_e, o, sources, put_send, False)


def cell_kernel(tau, last, place, *refs):
    thickness, flux, halo, area = refs[:4]
    side, refs = refs[4:10], refs[10:]
    if last:
        h_next, ext = refs
    else:
        send_c, (h_next, out, ext) = refs[:4], refs[4:]
    ext[:, : 48 * LANES] = flux[...]
    for j in range(4):
        ext[:, 48 * LANES + 512 * j : 48 * LANES + 512 * (j + 1)] = halo[:, j * place : j * place + 512]
    for o in range(2):

        def put(d, i, value):
            group = o * 8 + d
            rows, at = (TOP, LOW)[i], slice(group * LANES, (group + 1) * LANES)
            own = spread_row(area, pl.ds(group, 1), slice(None))
            h_next[rows, at] = thickness[rows, at] - tau * value / own

        gather(SIDE, side, o, both(ext), put, True)
    if not last:

        def put_h(d, i, value):
            out[8 * i : 8 * i + 8, d * LANES : (d + 1) * LANES] = value

        gather(SEND_C, send_c, 0, both(h_next), put_h, False)


def exchange_kernel(width, src, dst, send_sem, recv_sem):
    me = lax.axis_index("dom")
    count = lax.axis_size("dom")
    barrier = pltpu.get_barrier_semaphore()
    for offset in OFFSETS:
        peer = me + offset

        @pl.when((peer >= 0) & (peer < count))
        def _():
            pl.semaphore_signal(barrier, inc=1, device_id=(peer,), device_id_type=pl.DeviceIdType.MESH)

    pl.semaphore_wait(barrier, jnp.minimum(me, 2) + jnp.minimum(count - 1 - me, 2))

    def copy(place, peer):
        at = slice(place * width, (place + 1) * width)
        return pltpu.make_async_remote_copy(
            src_ref=src.at[:, at],
            dst_ref=dst.at[:, at],
            send_sem=send_sem.at[place],
            recv_sem=recv_sem.at[place],
            device_id=(peer,),
            device_id_type=pl.DeviceIdType.MESH,
        )

    for place, offset in enumerate(OFFSETS):
        peer, origin = me + offset, me - offset

        @pl.when((peer >= 0) & (peer < count))
        def _():
            copy(place, peer).start()

        @pl.when((origin < 0) | (origin >= count))
        def _():
            dst[:, place * width : (place + 1) * width] = jnp.zeros((16, width), jnp.float32)

    for place, offset in enumerate(OFFSETS):
        peer, origin = me + offset, me - offset

        @pl.when((peer >= 0) & (peer < count))
        def _():
            copy(place, peer).wait_send()

        @pl.when((origin >= 0) & (origin < count))
        def _():
            copy(place, origin).wait_recv()


def floats(*shape):
    return jax.ShapeDtypeStruct(shape, jnp.float32)


def whole(count):
    return [pl.BlockSpec(memory_space=VMEM)] * count


def local(kernel, name, args, in_specs, outs, out_specs, scratch):
    return pl.pallas_call(
        kernel,
        name=name,
        in_specs=in_specs,
        out_shape=outs,
        out_specs=out_specs,
        scratch_shapes=scratch,
        compiler_params=pltpu.CompilerParams(vmem_limit_bytes=48 << 20),
    )(*args)


def exchange(buffer):
    columns = buffer.shape[1]
    width = columns // 4
    return pl.pallas_call(
        functools.partial(exchange_kernel, width),
        name="exchange_halo",
        in_specs=whole(1),
        out_shape=floats(16, columns),
        out_specs=pl.BlockSpec(memory_space=VMEM),
        scratch_shapes=[pltpu.SemaphoreType.DMA((4,)), pltpu.SemaphoreType.DMA((4,))],
        compiler_params=pltpu.CompilerParams(collective_id=width // 256, has_side_effects=True),
    )(buffer)


def table_scratch(terms):
    return [VMEM((terms, 8, LANES), jnp.int32), VMEM((terms, 8, LANES), jnp.int32)]


def shards(
    thickness,
    velocity,
    send_cells,
    send_edges,
    cell_edges,
    cell_orient,
    edge_cells,
    edge_edges,
    edge_weights,
    cell_area,
    edge_spacing,
    edge_length,
    coriolis,
):
    made = local(
        sends_kernel,
        "plan_sends",
        (thickness, velocity, send_cells, send_edges),
        whole(4),
        SEND_E.shapes() + SEND_C.shapes() + [floats(16, 4 * 768)],
        SEND_E.out_specs() + SEND_C.out_specs() + whole(1),
        table_scratch(1) + [SMEM((8, LANES), jnp.int32), SMEM((8, LANES), jnp.int32)],
    )
    send_e, send_c, buffer = made[:4], made[4:8], made[8]
    made = local(
        plans_kernel,
        "plan_gathers",
        (edge_edges, edge_weights, edge_cells, cell_edges, cell_orient),
        whole(5),
        AROUND.shapes() + PAIR.shapes() + SIDE.shapes(),
        AROUND.out_specs() + PAIR.out_specs() + SIDE.out_specs(),
        table_scratch(10),
    )
    around, pair, side = made[:6], made[6:10], made[10:]
    halo_u = halo_h = exchange(buffer)
    u_place, h_place = (768, 0), (768, 512)
    h, u = thickness, velocity
    edge_coefs = [x.reshape(48, LANES) for x in (edge_spacing, edge_length, coriolis)]
    area = cell_area.reshape(16, LANES)
    for section in range(3):
        tau = time_step / (3 - section)
        last = section == 2
        width = 512 if last else 1024
        u, flux, buffer = local(
            functools.partial(edge_kernel, tau, last, u_place, h_place),
            "edge_section",
            (velocity, u, h, halo_u, halo_h, *edge_coefs, *around, *pair, *send_e),
            whole(8) + AROUND.in_specs() + PAIR.in_specs() + SEND_E.in_specs(),
            [floats(16, 48 * LANES), floats(16, 48 * LANES), floats(16, 4 * width)],
            whole(3),
            [
                VMEM((16, 64 * LANES), jnp.float32),
                VMEM((16, 24 * LANES), jnp.float32),
                VMEM((16, 8 * LANES), jnp.float32),
                VMEM((16, 8 * LANES), jnp.float32),
            ],
        )
        halo_u = exchange(buffer)
        u_place = (1024, 512)
        made = local(
            functools.partial(cell_kernel, tau, last, width),
            "cell_section",
            (thickness, flux, halo_u, area, *side) + (() if last else tuple(send_c)),
            whole(4) + SIDE.in_specs() + ([] if last else SEND_C.in_specs()),
            [floats(16, 16 * LANES)] + ([] if last else [floats(16, 8 * LANES)]),
            whole(1 if last else 2),
            [VMEM((16, 64 * LANES), jnp.float32)],
        )
        h = made[0]
        if not last:
            halo_h = exchange(made[1])
            h_place = (256, 0)
    return h, u


def solution(mesh):
    return jax.shard_map(
        shards,
        mesh=mesh,
        in_specs=(
            P(None, "dom"),
            P(None, "dom"),
            P("dom", None),
            P("dom", None),
            P(None, "dom"),
            P(None, "dom"),
            P(None, "dom"),
            P(None, "dom"),
            P(None, "dom"),
            P("dom"),
            P("dom"),
            P("dom"),
            P("dom"),
        ),
        out_specs=(P(None, "dom"), P(None, "dom")),
        check_vma=False,
    )
```

```python
import functools

import jax
import jax.numpy as jnp
from jax import lax
from jax.experimental import pallas as pl
from jax.experimental.pallas import tpu as pltpu
from jax.sharding import PartitionSpec as P

gravity = 0.1
mixing = 0.2
time_step = 0.5
LANES = 128
OFFSETS = (-2, -1, 1, 2)
VMEM = pltpu.VMEM
SMEM = pltpu.SMEM
TOP, LOW = slice(0, 8), slice(8, 16)


class Plan:
    rows = weights = ids = 0

    def __init__(self, terms, octets, first, chunks, cap, turns, cuts, weighted):
        self.terms, self.octets, self.first, self.chunks = terms, octets, first, chunks
        self.cap, self.turns, self.cuts, self.weighted = cap, turns, cuts, weighted
        self.row_at, self.weight_at, self.id_at = Plan.rows, Plan.weights, Plan.ids
        self.id_rows = -(-cap // LANES)
        Plan.rows += octets * cap
        Plan.weights += octets * cap * weighted
        Plan.ids += octets * self.id_rows


AROUND = Plan(10, 6, 0, 48, 272, 4, 2, True), Plan(10, 6, 48, 16, 104, 2, 1, True)
PAIR = Plan(1, 12, 0, 16, 56, 1, 1, False), Plan(1, 12, 16, 8, 32, 1, 1, False)
SIDE = Plan(6, 2, 0, 48, 208, 4, 2, True), Plan(6, 2, 48, 16, 80, 2, 1, True)
SEND_E = Plan(1, 2, 0, 48, 112, 2, 1, False)
SEND_C = Plan(1, 1, 0, 16, 64, 1, 1, False)
ROWS, WEIGHTS, IDS = Plan.rows, Plan.weights, -(-Plan.ids // 8) * 8


def iota(axis):
    return lax.broadcasted_iota(jnp.int32, (8, LANES), axis)


def spread(row):
    return jnp.broadcast_to(row, (8, LANES))


def turn(x, shift):
    return pltpu.roll(x, shift, 0)


def lanes_at(position):
    return pl.ds(pl.multiple_of(position * LANES, LANES), LANES)


def sums_of_rows(parts, sub):
    for bit in (1, 2, 4):
        first = (sub & bit) == 0
        parts = [jnp.where(first, a, b) + turn(jnp.where(first, b, a), bit) for a, b in zip(parts[::2], parts[1::2])]
    return parts[0]


def build(plan, raw, scale, packed, weights, ids, over, chunks, keys, loads):
    sub, lane = iota(0), iota(1)
    tiles = -(-plan.chunks // 8)
    numbers = [sub + 8 * v for v in range(tiles)]

    def octet(o, carry):
        at = pl.ds(pl.multiple_of(o * 8, 8), 8)
        for k in range(plan.terms):
            chunks[k] = lax.shift_right_logical(raw[k, at, :], 7) - plan.first

        def rank(k, counts):
            counts = list(counts)
            parts = []
            for s in range(8):
                chunk = spread(chunks[k, s : s + 1, :])
                part = None
                for v in range(tiles):
                    hit = chunk == numbers[v]
                    seen = jnp.where(hit, counts[v], 0)
                    part = seen if part is None else part + seen
                    counts[v] = jnp.where(hit, counts[v] + 1, counts[v])
                parts.append(part)
            keys[k] = sums_of_rows(parts, sub)
            return tuple(counts)

        counts = lax.fori_loop(0, plan.terms, rank, tuple(jnp.zeros((8, LANES), jnp.int32) for _ in range(tiles)))
        most = [spread(jnp.max(c, axis=1, keepdims=True)) for c in counts]
        upto = most
        for shift in (1, 2, 4):
            upto = [x + jnp.where(sub >= shift, turn(x, shift), 0) for x in upto]
        before = jnp.zeros((8, LANES), jnp.int32)
        starts = jnp.zeros((8, LANES), jnp.int32)
        for v in range(tiles):
            starts = starts + jnp.where(lane == numbers[v], upto[v] - most[v] + before, 0)
            before = before + spread(upto[v][7:8])
        for shift in (1, 2, 4):
            starts = starts + turn(starts, shift)
        over[...] = jnp.maximum(over[...], jnp.where(before > plan.cap, 1.0, 0.0))
        for k in range(plan.terms):
            chunk = chunks[k]
            inside = (chunk >= 0) & (chunk < plan.chunks)
            start = jnp.take_along_axis(starts, chunk & 127, axis=1, mode="promise_in_bounds")
            keys[k] = jnp.where(inside, start + keys[k], -1)
            loads[k] = (raw[k, at, :] & 127) | (sub << 7) | (jnp.where(inside, chunk, 0) << 11)
        places = [jnp.zeros((8, LANES), jnp.int32) for _ in range(plan.id_rows)]
        size = plan.cap // 8 // plan.cuts
        for cut in range(plan.cuts):
            tops = [8 * (cut * size + v) for v in range(size)]

            def match(k, found):
                load, weight = list(found[:size]), list(found[size:])
                for s in range(8):
                    wanted = spread(keys[k, s : s + 1, :])
                    value = spread(loads[k, s : s + 1, :])
                    if plan.weighted:
                        factor = spread(scale[k, pl.ds(o * 8 + s, 1), :])
                    for v in range(size):
                        here = wanted == sub + tops[v]
                        load[v] = jnp.where(here, value, load[v])
                        if plan.weighted:
                            weight[v] = jnp.where(here, factor, weight[v])
                return (*load, *weight)

            begin = [jnp.full((8, LANES), 8 << 7, jnp.int32)] * size
            begin += [jnp.zeros((8, LANES), jnp.float32)] * (size * plan.weighted)
            found = lax.fori_loop(0, plan.terms, match, tuple(begin))
            for v in range(size):
                load = found[v]
                offset = o * plan.cap + tops[v]
                packed[pl.ds(pl.multiple_of(plan.row_at + offset, 8), 8), :] = load & 2047
                if plan.weighted:
                    weights[pl.ds(pl.multiple_of(plan.weight_at + offset, 8), 8), :] = found[size + v]
                own = jnp.max(load >> 11, axis=1, keepdims=True)
                which = tops[v] // LANES
                places[which] = places[which] + jnp.where(lane == sub + tops[v] % LANES, own, 0)
        for i, place in enumerate(places):
            ids[pl.ds(plan.id_at + o * plan.id_rows + i, 1), :] = jnp.sum(place, axis=0, keepdims=True)
        return carry

    lax.fori_loop(0, plan.octets, octet, 0)


def plans_kernel(send_c, send_e, cell_edges, cell_orient, edge_cells, edge_edges, edge_weights, *rest):
    packed, weights, ids, over, around, factors, pair, side, signs, to_e, to_c, chunks, keys, loads = rest
    over[...] = jnp.zeros((8, LANES), jnp.float32)
    ids[...] = jnp.zeros((IDS, LANES), jnp.int32)
    for j in range(4):
        for q in range(4):
            to_e[0, 4 * j + q : 4 * j + q + 1, :] = send_e[j : j + 1, q * LANES : (q + 1) * LANES]
        for q in range(2):
            to_c[0, 2 * j + q : 2 * j + q + 1, :] = send_c[j : j + 1, q * LANES : (q + 1) * LANES]
    for g in range(48):
        at = slice(g * LANES, (g + 1) * LANES)
        for k in range(10):
            around[k, g : g + 1, :] = edge_edges[k : k + 1, at]
            factors[k, g : g + 1, :] = edge_weights[k : k + 1, at]
        for k in range(2):
            to = g // 4 * 8 + k * 4 + g % 4
            pair[0, to : to + 1, :] = edge_cells[k : k + 1, at]
    for g in range(16):
        at = slice(g * LANES, (g + 1) * LANES)
        for k in range(6):
            side[k, g : g + 1, :] = cell_edges[k : k + 1, at]
            signs[k, g : g + 1, :] = (2 * cell_orient[k : k + 1, at] - 1).astype(jnp.float32)
    tail = (packed, weights, ids, over, chunks, keys, loads)
    build(SEND_E, to_e, None, *tail)
    build(SEND_C, to_c, None, *tail)
    for i in range(2):
        build(AROUND[i], around, factors, *tail)
        build(PAIR[i], pair, None, *tail)
        build(SIDE[i], side, signs, *tail)


def gather(plan, lists, o, sources, sums):
    packed, weights, ids = lists
    steps = plan.cap // plan.turns

    def step(t, sums):
        sums = list(sums)
        for r in range(steps):
            row = t * steps + r
            at = o * plan.cap + row
            chunk = ids[plan.id_at + o * plan.id_rows + row // LANES, row % LANES]
            load = spread(packed[pl.ds(plan.row_at + at, 1), :])
            pick, goal = load & 127, lax.shift_right_logical(load, 7)
            found = [jnp.take_along_axis(take(chunk), pick, axis=1, mode="promise_in_bounds") for take in sources]
            if plan.weighted:
                factor = spread(weights[pl.ds(plan.weight_at + at, 1), :])
                found = [value * factor for value in found]
            for d in range(8):
                mine = goal == d
                for i, value in enumerate(found):
                    j = d * len(sources) + i
                    sums[j] = jnp.where(mine, sums[j] + value if plan.weighted else value, sums[j])
        return tuple(sums)

    return lax.fori_loop(0, plan.turns, step, tuple(sums))


def zeros(count):
    return [jnp.zeros((8, LANES), jnp.float32) for _ in range(count)]


def both(*takes):
    return [functools.partial(take, rows) for take in takes for rows in (TOP, LOW)]


def table(ref):
    return lambda rows, chunk: ref[chunk, rows, :]


FIELDS = 3


def step_kernel(thickness, velocity, packed_in, weights_in, spacing_in, length_in, coriolis_in, area_in, ids, *rest):
    h_out, u_out = rest[:2]
    (h0, u0, packed, weights, spacing, length, coriolis, area, loaded) = rest[2:11]
    (h, u, flux, tangent, cells, spread_sum, send_h, send_u, send_f, halo_h, halo_u, halo_f, near, sent, came) = rest[11:]
    me = lax.axis_index("dom")
    count = lax.axis_size("dom")
    barrier = pltpu.get_barrier_semaphore()
    for offset in OFFSETS:
        peer = me + offset

        @pl.when((peer >= 0) & (peer < count))
        def _():
            pl.semaphore_signal(barrier, inc=1, device_id=(peer,), device_id_type=pl.DeviceIdType.MESH)

    lists = (packed, weights, ids)
    given = (thickness, velocity, packed_in, spacing_in, length_in, coriolis_in, area_in, weights_in)
    kept = (h0, u0, packed, spacing, length, coriolis, area, weights)
    copies = [pltpu.make_async_copy(a, b, loaded.at[i]) for i, (a, b) in enumerate(zip(given, kept))]
    for copy in copies:
        copy.start()
    sends, halos = (send_h, send_u, send_f), (halo_h, halo_u, halo_f)
    widths = (2, 4, 4)

    def copy_of(field, k, place, peer):
        at = pl.ds(place * widths[field], widths[field])
        return pltpu.make_async_remote_copy(
            src_ref=sends[field].at[k, at],
            dst_ref=halos[field].at[k, at],
            send_sem=sent.at[k, field, place],
            recv_sem=came.at[k, field, place],
            device_id=(peer,),
            device_id_type=pl.DeviceIdType.MESH,
        )

    def start(field, k):
        for place, offset in enumerate(OFFSETS):
            peer = me + offset

            @pl.when((peer >= 0) & (peer < count))
            def _():
                copy_of(field, k, place, peer).start()

    def arrive(field, k):
        for place, offset in enumerate(OFFSETS):
            origin = me - offset

            @pl.when((origin >= 0) & (origin < count))
            def _():
                copy_of(field, k, place, origin).wait_recv()

        near[: 4 * widths[field]] = halos[field][k]

    for place, offset in enumerate(OFFSETS):
        origin = me - offset

        @pl.when((origin < 0) | (origin >= count))
        def _():
            for halo, width in zip(halos, widths):
                for k in range(3):
                    halo[k, place * width : (place + 1) * width] = jnp.zeros((width, 16, LANES), jnp.float32)

    def send_edges(k, *refs):
        sources = both(*(table(source) for source, _ in refs))

        def octet(o, carry):
            found = gather(SEND_E, lists, o, sources, zeros(8 * len(sources)))
            for d in range(8):
                for i, (_, buffer) in enumerate(refs):
                    for j, rows in enumerate((TOP, LOW)):
                        buffer[k, o * 8 + d, rows, :] = found[d * len(sources) + 2 * i + j]
            return carry

        lax.fori_loop(0, 2, octet, 0)

    def send_cells(k, source):
        found = gather(SEND_C, lists, 0, both(table(source)), zeros(16))
        for d in range(8):
            for j, rows in enumerate((TOP, LOW)):
                send_h[k, d, rows, :] = found[2 * d + j]

    for i in range(3):
        copies[i].wait()
    for group in range(48):
        u[group] = u0[:, group * LANES : (group + 1) * LANES]
    for group in range(16):
        h[group] = h0[:, group * LANES : (group + 1) * LANES]
    send_edges(0, (u, send_u))
    send_cells(0, h)
    pl.semaphore_wait(barrier, jnp.minimum(me, 2) + jnp.minimum(count - 1 - me, 2))
    start(0, 0)
    start(1, 0)
    for i in range(3, len(copies)):
        copies[i].wait()
    sub = iota(0)

    def running(x):
        for shift in (1, 2, 4):
            x = x + jnp.where(sub >= shift, turn(x, shift), 0.0)
        return x

    def sweep(plan, take, ref, fresh):
        def octet(o, carry):
            at = [o * 8 + d for d in range(8)]
            begin = zeros(16) if fresh else [ref[a, rows, :] for a in at for rows in (TOP, LOW)]
            found = gather(plan, lists, o, both(take), begin)
            for d in range(8):
                for j, rows in enumerate((TOP, LOW)):
                    ref[at[d], rows, :] = found[2 * d + j]
            return carry

        lax.fori_loop(0, plan.octets, octet, 0)

    def edges_of(k, tau):
        def quad(q, carry):
            for e in range(4):
                group = q * 4 + e
                at = lanes_at(group)
                left, right = q * 8 + e, q * 8 + 4 + e
                step = [cells[right, rows, :] - cells[left, rows, :] for rows in (TOP, LOW)]
                mean = [0.5 * (cells[right, rows, :] + cells[left, rows, :]) for rows in (TOP, LOW)]
                column = [running(x) for x in step]
                column[1] = column[1] + spread(column[0][7:8])
                pressure = [gravity * (c - 0.5 * x) for c, x in zip(column, step)]
                now = [u[group, rows, :] for rows in (TOP, LOW)]
                upper = [
                    jnp.where(sub == 0, now[0], turn(now[0], 1)),
                    jnp.where(sub == 0, spread(now[0][7:8]), turn(now[1], 1)),
                ]
                lower = [
                    jnp.where(sub == 7, spread(now[1][0:1]), turn(now[0], 7)),
                    jnp.where(sub == 7, now[1], turn(now[1], 7)),
                ]
                gap, long, spin = [spread(ref[pl.ds(group, 1), :]) for ref in (spacing, length, coriolis)]
                for i, rows in enumerate((TOP, LOW)):
                    mix = mixing * (upper[i] + lower[i] - 2.0 * now[i])
                    fresh = u0[rows, at] + tau * (-pressure[i] / gap + spin * tangent[group, rows, :] + mix)
                    u[group, rows, :] = fresh
                    flux[group, rows, :] = fresh * mean[i] * long
            return carry

        lax.fori_loop(0, 12, quad, 0)

    def section(k, carry):
        tau = time_step / (3 - k).astype(jnp.float32)
        sweep(AROUND[0], table(u), tangent, True)
        sweep(PAIR[0], table(h), cells, True)
        arrive(1, k)
        sweep(AROUND[1], table(near), tangent, False)
        arrive(0, k)
        sweep(PAIR[1], table(near), cells, False)
        edges_of(k, tau)

        later = jnp.minimum(k + 1, 2)

        @pl.when(k < 2)
        def _():
            send_edges_pair(k, later)
            start(2, k)
            start(1, later)

        @pl.when(k == 2)
        def _():
            send_edges(2, (flux, send_f))
            start(2, 2)

        sweep(SIDE[0], table(flux), spread_sum, True)
        arrive(2, k)
        sweep(SIDE[1], table(near), spread_sum, False)
        for group in range(16):
            at = slice(group * LANES, (group + 1) * LANES)
            own = spread(area[group : group + 1, :])
            for rows in (TOP, LOW):
                h[group, rows, :] = h0[rows, at] - tau * spread_sum[group, rows, :] / own

        @pl.when(k < 2)
        def _():
            send_cells(later, h)
            start(0, later)

        return carry

    def send_edges_pair(k, later):
        sources = both(table(flux), table(u))

        def octet(o, carry):
            found = gather(SEND_E, lists, o, sources, zeros(32))
            for d in range(8):
                at = o * 8 + d
                for j, rows in enumerate((TOP, LOW)):
                    send_f[k, at, rows, :] = found[4 * d + j]
                    send_u[later, at, rows, :] = found[4 * d + 2 + j]
            return carry

        lax.fori_loop(0, 2, octet, 0)

    lax.fori_loop(0, 3, section, 0)
    for group in range(48):
        u_out[:, group * LANES : (group + 1) * LANES] = u[group]
    for group in range(16):
        h_out[:, group * LANES : (group + 1) * LANES] = h[group]
    for field in range(FIELDS):
        for k in range(3):
            for place, offset in enumerate(OFFSETS):
                peer = me + offset

                @pl.when((peer >= 0) & (peer < count))
                def _():
                    copy_of(field, k, place, peer).wait_send()


def floats(*shape):
    return jax.ShapeDtypeStruct(shape, jnp.float32)


def ints(*shape):
    return jax.ShapeDtypeStruct(shape, jnp.int32)


def whole(count):
    return [pl.BlockSpec(memory_space=VMEM)] * count


def held(dtype, *shapes):
    return [VMEM(shape, dtype) for shape in shapes]


def shifted(block, axis, distance):
    devices = range(lax.axis_size(axis))
    route = [(i - distance, i) for i in devices if i - distance in devices]
    return lax.ppermute(block, axis, route)


def peer_offsets(slot_count):
    half = slot_count // 2
    return [place - half if place < half else place - half + 1 for place in range(slot_count)]


def state_halo(cell_blocks, edge_blocks):
    slot_count = cell_blocks.shape[0]
    offsets = peer_offsets(slot_count)
    arrived = {}
    for place, offset in enumerate(offsets):
        arrived[offset] = shifted((cell_blocks[place], edge_blocks[place]), "dom", offset)
    cell_parts = [arrived[offset][0] for offset in offsets]
    edge_parts = [arrived[offset][1] for offset in offsets]
    return (jnp.concatenate(cell_parts, axis=0), jnp.concatenate(edge_parts, axis=0))


def flux_halo(flux_blocks):
    slot_count = flux_blocks.shape[0]
    offsets = peer_offsets(slot_count)
    arrived = {}
    for place, offset in enumerate(offsets):
        arrived[offset] = shifted(flux_blocks[place], "dom", offset)
    return jnp.concatenate([arrived[offset] for offset in offsets], axis=0)


def general(
    thickness,
    velocity,
    send_cells,
    send_edges,
    cell_edges,
    cell_orient,
    edge_cells,
    edge_edges,
    edge_weights,
    cell_area,
    edge_spacing,
    edge_length,
    coriolis,
):
    levels = thickness.shape[0]
    edge_count = velocity.shape[1]
    cell_count = thickness.shape[1]
    signs = (2 * cell_orient - 1).astype(jnp.float32).T
    pair_index = edge_cells.reshape(-1)
    around_index = edge_edges.reshape(-1)
    side_index = cell_edges.T.reshape(-1)
    rows_h0 = thickness.T
    rows_u0 = velocity.T
    rows_h = rows_h0
    rows_u = rows_u0
    for section in range(3):
        step_size = time_step / (3 - section)
        cell_blocks = jnp.take(rows_h, send_cells, axis=0)
        edge_blocks = jnp.take(rows_u, send_edges, axis=0)
        halo_h, halo_u = state_halo(cell_blocks, edge_blocks)
        ext_h = jnp.concatenate([rows_h, halo_h], axis=0)
        ext_u = jnp.concatenate([rows_u, halo_u], axis=0)
        ext_p = gravity * (jnp.cumsum(ext_h, axis=1) - 0.5 * ext_h)
        table = jnp.concatenate([ext_h, ext_p], axis=1)
        picked = jnp.take(table, pair_index, axis=0).reshape(2, edge_count, 2 * levels)
        left_h = picked[0, :, :levels]
        right_h = picked[1, :, :levels]
        gradient = (picked[1, :, levels:] - picked[0, :, levels:]) / edge_spacing[:, None]
        beside_all = jnp.take(ext_u, around_index, axis=0).reshape(-1, edge_count, levels)
        tangent = jnp.sum(beside_all * edge_weights[:, :, None], axis=0)
        upper = jnp.concatenate([rows_u[:, :1], rows_u[:, :-1]], axis=1)
        lower = jnp.concatenate([rows_u[:, 1:], rows_u[:, -1:]], axis=1)
        blend = mixing * (upper + lower - 2.0 * rows_u)
        u_next = rows_u0 + step_size * (-gradient + coriolis[:, None] * tangent + blend)
        flux = u_next * 0.5 * (left_h + right_h) * edge_length[:, None]
        halo_f = flux_halo(jnp.take(flux, send_edges, axis=0))
        ext_f = jnp.concatenate([flux, halo_f], axis=0)
        sides = jnp.take(ext_f, side_index, axis=0).reshape(cell_count, -1, levels)
        spread = jnp.sum(sides * signs[:, :, None], axis=1)
        rows_h = rows_h0 - step_size * spread / cell_area[:, None]
        rows_u = u_next
    return (rows_h.T, rows_u.T)


def shards(
    thickness,
    velocity,
    send_cells,
    send_edges,
    cell_edges,
    cell_orient,
    edge_cells,
    edge_edges,
    edge_weights,
    cell_area,
    edge_spacing,
    edge_length,
    coriolis,
):
    index = (send_cells, send_edges, cell_edges, cell_orient, edge_cells, edge_edges)
    around, side = (10, 48, LANES), (6, 16, LANES)
    packed, weights, ids, over = pl.pallas_call(
        plans_kernel,
        name="plan_gathers",
        in_specs=whole(7),
        out_shape=[ints(ROWS, LANES), floats(WEIGHTS, LANES), ints(IDS, LANES), floats(8, LANES)],
        out_specs=whole(4),
        scratch_shapes=held(jnp.int32, around)
        + held(jnp.float32, around)
        + held(jnp.int32, (1, 96, LANES), side)
        + held(jnp.float32, side)
        + held(jnp.int32, (1, 16, LANES), (1, 8, LANES), *[(10, 8, LANES)] * 3),
        compiler_params=pltpu.CompilerParams(vmem_limit_bytes=24 << 20),
    )(*index, edge_weights)
    overs = lax.psum(over[:1], "dom")[0, 0]
    coefs = [x.reshape(48, LANES) for x in (edge_spacing, edge_length, coriolis)] + [cell_area.reshape(16, LANES)]
    rows, groups, halo = (48, LANES), (48, 16, LANES), (3, 16, 16, LANES)
    fast = pl.pallas_call(
        step_kernel,
        name="three_sections",
        in_specs=[pl.BlockSpec(memory_space=pl.ANY)] * 8 + [pl.BlockSpec(memory_space=SMEM)],
        out_shape=[floats(16, 16 * LANES), floats(16, 48 * LANES)],
        out_specs=whole(2),
        scratch_shapes=held(jnp.float32, (16, 16 * LANES), (16, 48 * LANES))
        + held(jnp.int32, (ROWS, LANES))
        + held(jnp.float32, (WEIGHTS, LANES), rows, rows, rows, (16, LANES))
        + [pltpu.SemaphoreType.DMA((8,))]
        + held(jnp.float32, (16, 16, LANES), groups, groups, groups, (96, 16, LANES), (16, 16, LANES))
        + held(jnp.float32, (3, 8, 16, LANES), halo, halo, (3, 8, 16, LANES), halo, halo, (16, 16, LANES))
        + [pltpu.SemaphoreType.DMA((3, FIELDS, 4)), pltpu.SemaphoreType.DMA((3, FIELDS, 4))],
        compiler_params=pltpu.CompilerParams(collective_id=0, has_side_effects=True, vmem_limit_bytes=32 << 20),
    )(thickness, velocity, packed, weights, *coefs, ids)

    def in_general():
        return general(thickness, velocity, *index, edge_weights, cell_area, edge_spacing, edge_length, coriolis)

    return lax.cond(overs > 0, in_general, lambda: tuple(fast))


def solution(mesh):
    return jax.shard_map(
        shards,
        mesh=mesh,
        in_specs=(
            P(None, "dom"),
            P(None, "dom"),
            P("dom", None),
            P("dom", None),
            P(None, "dom"),
            P(None, "dom"),
            P(None, "dom"),
            P(None, "dom"),
            P(None, "dom"),
            P("dom"),
            P("dom"),
            P("dom"),
            P("dom"),
        ),
        out_specs=(P(None, "dom"), P(None, "dom")),
        check_vma=False,
    )
```

```python
import functools

import jax
import jax.numpy as jnp
from jax import lax
from jax.experimental import pallas as pl
from jax.experimental.pallas import tpu as pltpu
from jax.sharding import PartitionSpec as P

gravity = 0.1
mixing = 0.2
time_step = 0.5
LANES = 128
TILES = 12
OFFSETS = (-2, -1, 1, 2)
VMEM = pltpu.VMEM
SMEM = pltpu.SMEM
TOP, LOW = slice(0, 8), slice(8, 16)


class Plan:
    rows = weights = ids = 0

    def __init__(self, terms, octets, first, chunks, cap, turns, weighted, apart):
        self.terms, self.octets, self.first, self.chunks = terms, octets, first, chunks
        self.cap, self.turns, self.weighted, self.apart = cap, turns, weighted, apart
        self.goals = 8 * terms if apart else 8
        self.row_at, self.weight_at, self.id_at = Plan.rows, Plan.weights, Plan.ids
        self.id_rows = -(-cap // LANES)
        Plan.rows += octets * cap
        Plan.weights += octets * cap * weighted
        Plan.ids += octets * self.id_rows


AROUND = Plan(10, 6, 0, 48, 272, 4, True, False), Plan(10, 6, 48, 16, 104, 2, True, False)
PAIR = Plan(2, 6, 0, 16, 72, 1, False, True), Plan(2, 6, 16, 8, 40, 1, False, True)
SIDE = Plan(6, 2, 0, 48, 208, 4, True, False), Plan(6, 2, 48, 16, 80, 2, True, False)
SEND_E = Plan(1, 2, 0, 48, 112, 2, False, False)
SEND_C = Plan(1, 1, 0, 16, 64, 1, False, False)
ROWS, WEIGHTS, IDS = Plan.rows, Plan.weights, -(-Plan.ids // 8) * 8


def iota(axis):
    return lax.broadcasted_iota(jnp.int32, (8, LANES), axis)


def spread(row):
    return jnp.broadcast_to(row, (8, LANES))


def turn(x, shift):
    return pltpu.roll(x, shift, 0)


def lanes_at(position):
    return pl.ds(pl.multiple_of(position * LANES, LANES), LANES)


def sums_of_rows(parts, sub):
    for bit in (1, 2, 4):
        first = (sub & bit) == 0
        parts = [jnp.where(first, a, b) + turn(jnp.where(first, b, a), bit) for a, b in zip(parts[::2], parts[1::2])]
    return parts[0]


def build(plan, raw, scale, packed, weights, ids, over, chunks, keys, loads):
    sub, lane = iota(0), iota(1)
    tiles = -(-plan.chunks // 8)
    numbers = [sub + 8 * v for v in range(tiles)]

    def octet(o, carry):
        at = pl.ds(pl.multiple_of(o * 8, 8), 8)
        for k in range(plan.terms):
            chunks[k] = lax.shift_right_logical(raw[k, at, :], 7) - plan.first

        counts = [jnp.zeros((8, LANES), jnp.int32) for _ in range(tiles)]
        for k in range(plan.terms):
            parts = []
            for s in range(8):
                chunk = spread(chunks[k, s : s + 1, :])
                part = None
                for v in range(tiles):
                    hit = chunk == numbers[v]
                    seen = jnp.where(hit, counts[v], 0)
                    part = seen if part is None else part + seen
                    counts[v] = jnp.where(hit, counts[v] + 1, counts[v])
                parts.append(part)
            keys[k] = sums_of_rows(parts, sub)
        most = [spread(jnp.max(c, axis=1, keepdims=True)) for c in counts]
        upto = most
        for shift in (1, 2, 4):
            upto = [x + jnp.where(sub >= shift, turn(x, shift), 0) for x in upto]
        before = jnp.zeros((8, LANES), jnp.int32)
        starts = jnp.zeros((8, LANES), jnp.int32)
        for v in range(tiles):
            starts = starts + jnp.where(lane == numbers[v], upto[v] - most[v] + before, 0)
            before = before + spread(upto[v][7:8])
        for shift in (1, 2, 4):
            starts = starts + turn(starts, shift)
        over[...] = jnp.maximum(over[...], jnp.where(before > plan.cap, 1.0, 0.0))
        for k in range(plan.terms):
            chunk = chunks[k]
            inside = (chunk >= 0) & (chunk < plan.chunks)
            start = jnp.take_along_axis(starts, chunk & 127, axis=1, mode="promise_in_bounds")
            keys[k] = jnp.where(inside, start + keys[k], -1)
            loads[k] = (raw[k, at, :] & 127) | ((sub + 8 * k * plan.apart) << 7) | (jnp.where(inside, chunk, 0) << 12)
        places = [jnp.zeros((8, LANES), jnp.int32) for _ in range(plan.id_rows)]
        for top in range(0, plan.cap, 8 * TILES):
            tops = list(range(top, min(top + 8 * TILES, plan.cap), 8))
            size = len(tops)

            def match(k, found, tops=tops, size=size):
                load, weight = list(found[:size]), list(found[size:])
                for s in range(8):
                    wanted = spread(keys[k, s : s + 1, :])
                    value = spread(loads[k, s : s + 1, :])
                    if plan.weighted:
                        factor = spread(scale[k, pl.ds(o * 8 + s, 1), :])
                    for v in range(size):
                        here = wanted == sub + tops[v]
                        load[v] = jnp.where(here, value, load[v])
                        if plan.weighted:
                            weight[v] = jnp.where(here, factor, weight[v])
                return (*load, *weight)

            begin = [jnp.full((8, LANES), 16 << 7, jnp.int32)] * size
            begin += [jnp.zeros((8, LANES), jnp.float32)] * (size * plan.weighted)
            found = lax.fori_loop(0, plan.terms, match, tuple(begin))
            for v in range(size):
                load = found[v]
                offset = o * plan.cap + tops[v]
                packed[pl.ds(pl.multiple_of(plan.row_at + offset, 8), 8), :] = load & 4095
                if plan.weighted:
                    weights[pl.ds(pl.multiple_of(plan.weight_at + offset, 8), 8), :] = found[size + v]
                own = jnp.max(load >> 12, axis=1, keepdims=True)
                which = tops[v] // LANES
                places[which] = places[which] + jnp.where(lane == sub + tops[v] % LANES, own, 0)
        for i, place in enumerate(places):
            ids[pl.ds(plan.id_at + o * plan.id_rows + i, 1), :] = jnp.sum(place, axis=0, keepdims=True)
        return carry

    lax.fori_loop(0, plan.octets, octet, 0)


def plans_kernel(send_c, send_e, cell_edges, cell_orient, edge_cells, edge_edges, edge_weights, *rest):
    packed, weights, ids, over, around, factors, pair, side, signs, to_e, to_c, chunks, keys, loads = rest
    over[...] = jnp.zeros((8, LANES), jnp.float32)
    ids[...] = jnp.zeros((IDS, LANES), jnp.int32)
    for j in range(4):
        for q in range(4):
            to_e[0, 4 * j + q : 4 * j + q + 1, :] = send_e[j : j + 1, q * LANES : (q + 1) * LANES]
        for q in range(2):
            to_c[0, 2 * j + q : 2 * j + q + 1, :] = send_c[j : j + 1, q * LANES : (q + 1) * LANES]
    for g in range(48):
        at = slice(g * LANES, (g + 1) * LANES)
        for k in range(10):
            around[k, g : g + 1, :] = edge_edges[k : k + 1, at]
            factors[k, g : g + 1, :] = edge_weights[k : k + 1, at]
        for k in range(2):
            pair[k, g : g + 1, :] = edge_cells[k : k + 1, at]
    for g in range(16):
        at = slice(g * LANES, (g + 1) * LANES)
        for k in range(6):
            side[k, g : g + 1, :] = cell_edges[k : k + 1, at]
            signs[k, g : g + 1, :] = (2 * cell_orient[k : k + 1, at] - 1).astype(jnp.float32)
    tail = (packed, weights, ids, over, chunks, keys, loads)
    build(SEND_E, to_e, None, *tail)
    build(SEND_C, to_c, None, *tail)
    for i in range(2):
        build(AROUND[i], around, factors, *tail)
        build(PAIR[i], pair, None, *tail)
        build(SIDE[i], side, signs, *tail)


def gather(plan, lists, o, sources, sums):
    packed, weights, ids = lists
    steps = plan.cap // plan.turns

    def step(t, sums):
        sums = list(sums)
        for r in range(steps):
            row = t * steps + r
            at = o * plan.cap + row
            chunk = ids[plan.id_at + o * plan.id_rows + row // LANES, row % LANES]
            load = spread(packed[pl.ds(plan.row_at + at, 1), :])
            pick, goal = load & 127, lax.shift_right_logical(load, 7)
            found = [jnp.take_along_axis(take(chunk), pick, axis=1, mode="promise_in_bounds") for take in sources]
            if plan.weighted:
                factor = spread(weights[pl.ds(plan.weight_at + at, 1), :])
                found = [value * factor for value in found]
            for d in range(plan.goals):
                mine = goal == d
                for i, value in enumerate(found):
                    j = d * len(sources) + i
                    sums[j] = jnp.where(mine, sums[j] + value if plan.weighted else value, sums[j])
        return tuple(sums)

    return lax.fori_loop(0, plan.turns, step, tuple(sums))


def zeros(count):
    return [jnp.zeros((8, LANES), jnp.float32) for _ in range(count)]


def both(*takes):
    return [functools.partial(take, rows) for take in takes for rows in (TOP, LOW)]


def table(ref):
    return lambda rows, chunk: ref[chunk, rows, :]


FIELDS = 3


def partner(me, b):
    return me + b - 2 * b * (me // b % 2)


def step_kernel(thickness, velocity, packed_in, weights_in, spacing_in, length_in, coriolis_in, area_in, over, ids, *rest):
    h_out, u_out, mark = rest[:3]
    (h0, u0, packed, weights, spacing, length, coriolis, area, loaded) = rest[3:12]
    (h, u, flux, tangent, cells, spread_sum, send_h, send_u, send_f, halo_h, halo_u, halo_f, near, sent, came) = rest[12:27]
    told, heard, told_sem, heard_sem = rest[27:]
    me = lax.axis_index("dom")
    count = lax.axis_size("dom")
    barrier = pltpu.get_barrier_semaphore()
    for offset in OFFSETS:
        peer = me + offset

        @pl.when((peer >= 0) & (peer < count))
        def _():
            pl.semaphore_signal(barrier, inc=1, device_id=(peer,), device_id_type=pl.DeviceIdType.MESH)

    rounds = count.bit_length() - 1
    for r in range(2, rounds):
        pl.semaphore_signal(barrier, inc=1, device_id=(partner(me, 2**r),), device_id_type=pl.DeviceIdType.MESH)
    mark[...] = over[...]

    def tell(r):
        return pltpu.make_async_remote_copy(
            src_ref=told.at[r],
            dst_ref=heard.at[r],
            send_sem=told_sem.at[r],
            recv_sem=heard_sem.at[r],
            device_id=(partner(me, lax.shift_left(1, r)),),
            device_id_type=pl.DeviceIdType.MESH,
        )

    def spread_mark(r):
        @pl.when((r >= 1) & (r <= rounds))
        def _():
            tell(r - 1).wait_recv()
            mark[...] = jnp.maximum(mark[...], heard[r - 1])

        @pl.when(r < rounds)
        def _():
            told[r] = mark[...]
            tell(r).start()

    lists = (packed, weights, ids)
    given = (thickness, velocity, packed_in, spacing_in, length_in, coriolis_in, area_in, weights_in)
    kept = (h0, u0, packed, spacing, length, coriolis, area, weights)
    copies = [pltpu.make_async_copy(a, b, loaded.at[i]) for i, (a, b) in enumerate(zip(given, kept))]
    for copy in copies:
        copy.start()
    sends, halos = (send_h, send_u, send_f), (halo_h, halo_u, halo_f)
    widths = (2, 4, 4)

    def copy_of(field, k, place, peer):
        at = pl.ds(place * widths[field], widths[field])
        return pltpu.make_async_remote_copy(
            src_ref=sends[field].at[k, at],
            dst_ref=halos[field].at[k, at],
            send_sem=sent.at[k, field, place],
            recv_sem=came.at[k, field, place],
            device_id=(peer,),
            device_id_type=pl.DeviceIdType.MESH,
        )

    def start(field, k):
        for place, offset in enumerate(OFFSETS):
            peer = me + offset

            @pl.when((peer >= 0) & (peer < count))
            def _():
                copy_of(field, k, place, peer).start()

    def arrive(field, k):
        for place, offset in enumerate(OFFSETS):
            origin = me - offset

            @pl.when((origin >= 0) & (origin < count))
            def _():
                copy_of(field, k, place, origin).wait_recv()

        near[: 4 * widths[field]] = halos[field][k]

    for place, offset in enumerate(OFFSETS):
        origin = me - offset

        @pl.when((origin < 0) | (origin >= count))
        def _():
            for halo, width in zip(halos, widths):
                for k in range(3):
                    halo[k, place * width : (place + 1) * width] = jnp.zeros((width, 16, LANES), jnp.float32)

    def send_edges(k, *refs):
        sources = both(*(table(source) for source, _ in refs))

        def octet(o, carry):
            found = gather(SEND_E, lists, o, sources, zeros(8 * len(sources)))
            for d in range(8):
                for i, (_, buffer) in enumerate(refs):
                    for j, rows in enumerate((TOP, LOW)):
                        buffer[k, o * 8 + d, rows, :] = found[d * len(sources) + 2 * i + j]
            return carry

        lax.fori_loop(0, 2, octet, 0)

    def send_cells(k, source):
        found = gather(SEND_C, lists, 0, both(table(source)), zeros(16))
        for d in range(8):
            for j, rows in enumerate((TOP, LOW)):
                send_h[k, d, rows, :] = found[2 * d + j]

    for i in range(3):
        copies[i].wait()
    for group in range(48):
        u[group] = u0[:, group * LANES : (group + 1) * LANES]
    for group in range(16):
        h[group] = h0[:, group * LANES : (group + 1) * LANES]
    send_edges(0, (u, send_u))
    send_cells(0, h)
    pl.semaphore_wait(barrier, jnp.minimum(me, 2) + jnp.minimum(count - 1 - me, 2) + max(rounds - 2, 0))
    start(0, 0)
    start(1, 0)
    for i in range(3, len(copies)):
        copies[i].wait()
    sub = iota(0)

    def running(x):
        for shift in (1, 2, 4):
            x = x + jnp.where(sub >= shift, turn(x, shift), 0.0)
        return x

    def sweep(plan, take, ref, fresh):
        def octet(o, carry):
            at = [o * 8 + d % 8 + d // 8 * 48 for d in range(plan.goals)]
            begin = zeros(2 * plan.goals) if fresh else [ref[a, rows, :] for a in at for rows in (TOP, LOW)]
            found = gather(plan, lists, o, both(take), begin)
            for d in range(plan.goals):
                for j, rows in enumerate((TOP, LOW)):
                    ref[at[d], rows, :] = found[2 * d + j]
            return carry

        lax.fori_loop(0, plan.octets, octet, 0)

    def edges_of(k, tau):
        def quad(q, carry):
            for e in range(4):
                group = q * 4 + e
                at = lanes_at(group)
                left, right = group, 48 + group
                step = [cells[right, rows, :] - cells[left, rows, :] for rows in (TOP, LOW)]
                mean = [0.5 * (cells[right, rows, :] + cells[left, rows, :]) for rows in (TOP, LOW)]
                column = [running(x) for x in step]
                column[1] = column[1] + spread(column[0][7:8])
                pressure = [gravity * (c - 0.5 * x) for c, x in zip(column, step)]
                now = [u[group, rows, :] for rows in (TOP, LOW)]
                upper = [
                    jnp.where(sub == 0, now[0], turn(now[0], 1)),
                    jnp.where(sub == 0, spread(now[0][7:8]), turn(now[1], 1)),
                ]
                lower = [
                    jnp.where(sub == 7, spread(now[1][0:1]), turn(now[0], 7)),
                    jnp.where(sub == 7, now[1], turn(now[1], 7)),
                ]
                gap, long, spin = [spread(ref[pl.ds(group, 1), :]) for ref in (spacing, length, coriolis)]
                for i, rows in enumerate((TOP, LOW)):
                    mix = mixing * (upper[i] + lower[i] - 2.0 * now[i])
                    fresh = u0[rows, at] + tau * (-pressure[i] / gap + spin * tangent[group, rows, :] + mix)
                    u[group, rows, :] = fresh
                    flux[group, rows, :] = fresh * mean[i] * long
            return carry

        lax.fori_loop(0, 12, quad, 0)

    def section(k, carry):
        tau = time_step / (3 - k).astype(jnp.float32)
        spread_mark(3 * k)
        sweep(AROUND[0], table(u), tangent, True)
        sweep(PAIR[0], table(h), cells, True)
        arrive(1, k)
        sweep(AROUND[1], table(near), tangent, False)
        arrive(0, k)
        sweep(PAIR[1], table(near), cells, False)
        spread_mark(3 * k + 1)
        edges_of(k, tau)

        later = jnp.minimum(k + 1, 2)

        @pl.when(k < 2)
        def _():
            send_edges_pair(k, later)
            start(2, k)
            start(1, later)

        @pl.when(k == 2)
        def _():
            send_edges(2, (flux, send_f))
            start(2, 2)

        sweep(SIDE[0], table(flux), spread_sum, True)
        spread_mark(3 * k + 2)
        arrive(2, k)
        sweep(SIDE[1], table(near), spread_sum, False)
        for group in range(16):
            at = slice(group * LANES, (group + 1) * LANES)
            own = spread(area[group : group + 1, :])
            for rows in (TOP, LOW):
                h[group, rows, :] = h0[rows, at] - tau * spread_sum[group, rows, :] / own

        @pl.when(k < 2)
        def _():
            send_cells(later, h)
            start(0, later)

        return carry

    def send_edges_pair(k, later):
        sources = both(table(flux), table(u))

        def octet(o, carry):
            found = gather(SEND_E, lists, o, sources, zeros(32))
            for d in range(8):
                at = o * 8 + d
                for j, rows in enumerate((TOP, LOW)):
                    send_f[k, at, rows, :] = found[4 * d + j]
                    send_u[later, at, rows, :] = found[4 * d + 2 + j]
            return carry

        lax.fori_loop(0, 2, octet, 0)

    lax.fori_loop(0, 3, section, 0)
    for group in range(48):
        u_out[:, group * LANES : (group + 1) * LANES] = u[group]
    for group in range(16):
        h_out[:, group * LANES : (group + 1) * LANES] = h[group]
    for r in range(rounds):
        tell(r).wait_send()
    for field in range(FIELDS):
        for k in range(3):
            for place, offset in enumerate(OFFSETS):
                peer = me + offset

                @pl.when((peer >= 0) & (peer < count))
                def _():
                    copy_of(field, k, place, peer).wait_send()


def floats(*shape):
    return jax.ShapeDtypeStruct(shape, jnp.float32)


def ints(*shape):
    return jax.ShapeDtypeStruct(shape, jnp.int32)


def whole(count):
    return [pl.BlockSpec(memory_space=VMEM)] * count


def held(dtype, *shapes):
    return [VMEM(shape, dtype) for shape in shapes]


def shifted(block, axis, distance):
    devices = range(lax.axis_size(axis))
    route = [(i - distance, i) for i in devices if i - distance in devices]
    return lax.ppermute(block, axis, route)


def peer_offsets(slot_count):
    half = slot_count // 2
    return [place - half if place < half else place - half + 1 for place in range(slot_count)]


def state_halo(cell_blocks, edge_blocks):
    slot_count = cell_blocks.shape[0]
    offsets = peer_offsets(slot_count)
    arrived = {}
    for place, offset in enumerate(offsets):
        arrived[offset] = shifted((cell_blocks[place], edge_blocks[place]), "dom", offset)
    cell_parts = [arrived[offset][0] for offset in offsets]
    edge_parts = [arrived[offset][1] for offset in offsets]
    return (jnp.concatenate(cell_parts, axis=0), jnp.concatenate(edge_parts, axis=0))


def flux_halo(flux_blocks):
    slot_count = flux_blocks.shape[0]
    offsets = peer_offsets(slot_count)
    arrived = {}
    for place, offset in enumerate(offsets):
        arrived[offset] = shifted(flux_blocks[place], "dom", offset)
    return jnp.concatenate([arrived[offset] for offset in offsets], axis=0)


def general(
    thickness,
    velocity,
    send_cells,
    send_edges,
    cell_edges,
    cell_orient,
    edge_cells,
    edge_edges,
    edge_weights,
    cell_area,
    edge_spacing,
    edge_length,
    coriolis,
):
    levels = thickness.shape[0]
    edge_count = velocity.shape[1]
    cell_count = thickness.shape[1]
    signs = (2 * cell_orient - 1).astype(jnp.float32).T
    pair_index = edge_cells.reshape(-1)
    around_index = edge_edges.reshape(-1)
    side_index = cell_edges.T.reshape(-1)
    rows_h0 = thickness.T
    rows_u0 = velocity.T
    rows_h = rows_h0
    rows_u = rows_u0
    for section in range(3):
        step_size = time_step / (3 - section)
        cell_blocks = jnp.take(rows_h, send_cells, axis=0)
        edge_blocks = jnp.take(rows_u, send_edges, axis=0)
        halo_h, halo_u = state_halo(cell_blocks, edge_blocks)
        ext_h = jnp.concatenate([rows_h, halo_h], axis=0)
        ext_u = jnp.concatenate([rows_u, halo_u], axis=0)
        ext_p = gravity * (jnp.cumsum(ext_h, axis=1) - 0.5 * ext_h)
        table = jnp.concatenate([ext_h, ext_p], axis=1)
        picked = jnp.take(table, pair_index, axis=0).reshape(2, edge_count, 2 * levels)
        left_h = picked[0, :, :levels]
        right_h = picked[1, :, :levels]
        gradient = (picked[1, :, levels:] - picked[0, :, levels:]) / edge_spacing[:, None]
        beside_all = jnp.take(ext_u, around_index, axis=0).reshape(-1, edge_count, levels)
        tangent = jnp.sum(beside_all * edge_weights[:, :, None], axis=0)
        upper = jnp.concatenate([rows_u[:, :1], rows_u[:, :-1]], axis=1)
        lower = jnp.concatenate([rows_u[:, 1:], rows_u[:, -1:]], axis=1)
        blend = mixing * (upper + lower - 2.0 * rows_u)
        u_next = rows_u0 + step_size * (-gradient + coriolis[:, None] * tangent + blend)
        flux = u_next * 0.5 * (left_h + right_h) * edge_length[:, None]
        halo_f = flux_halo(jnp.take(flux, send_edges, axis=0))
        ext_f = jnp.concatenate([flux, halo_f], axis=0)
        sides = jnp.take(ext_f, side_index, axis=0).reshape(cell_count, -1, levels)
        spread = jnp.sum(sides * signs[:, :, None], axis=1)
        rows_h = rows_h0 - step_size * spread / cell_area[:, None]
        rows_u = u_next
    return (rows_h.T, rows_u.T)


def shards(
    thickness,
    velocity,
    send_cells,
    send_edges,
    cell_edges,
    cell_orient,
    edge_cells,
    edge_edges,
    edge_weights,
    cell_area,
    edge_spacing,
    edge_length,
    coriolis,
):
    index = (send_cells, send_edges, cell_edges, cell_orient, edge_cells, edge_edges)
    around, side = (10, 48, LANES), (6, 16, LANES)
    packed, weights, ids, over = pl.pallas_call(
        plans_kernel,
        name="plan_gathers",
        in_specs=whole(7),
        out_shape=[ints(ROWS, LANES), floats(WEIGHTS, LANES), ints(IDS, LANES), floats(8, LANES)],
        out_specs=whole(4),
        scratch_shapes=held(jnp.int32, around)
        + held(jnp.float32, around)
        + held(jnp.int32, (2, 48, LANES), side)
        + held(jnp.float32, side)
        + held(jnp.int32, (1, 16, LANES), (1, 8, LANES), *[(10, 8, LANES)] * 3),
        compiler_params=pltpu.CompilerParams(vmem_limit_bytes=24 << 20),
    )(*index, edge_weights)
    coefs = [x.reshape(48, LANES) for x in (edge_spacing, edge_length, coriolis)] + [cell_area.reshape(16, LANES)]
    rows, groups, halo = (48, LANES), (48, 16, LANES), (3, 16, 16, LANES)
    h, u, mark = pl.pallas_call(
        step_kernel,
        name="three_sections",
        in_specs=[pl.BlockSpec(memory_space=pl.ANY)] * 8 + whole(1) + [pl.BlockSpec(memory_space=SMEM)],
        out_shape=[floats(16, 16 * LANES), floats(16, 48 * LANES), floats(8, LANES)],
        out_specs=whole(3),
        scratch_shapes=held(jnp.float32, (16, 16 * LANES), (16, 48 * LANES))
        + held(jnp.int32, (ROWS, LANES))
        + held(jnp.float32, (WEIGHTS, LANES), rows, rows, rows, (16, LANES))
        + [pltpu.SemaphoreType.DMA((8,))]
        + held(jnp.float32, (16, 16, LANES), groups, groups, groups, (96, 16, LANES), (16, 16, LANES))
        + held(jnp.float32, (3, 8, 16, LANES), halo, halo, (3, 8, 16, LANES), halo, halo, (16, 16, LANES))
        + [pltpu.SemaphoreType.DMA((3, FIELDS, 4)), pltpu.SemaphoreType.DMA((3, FIELDS, 4))]
        + held(jnp.float32, (7, 8, LANES), (7, 8, LANES))
        + [pltpu.SemaphoreType.DMA((7,)), pltpu.SemaphoreType.DMA((7,))],
        compiler_params=pltpu.CompilerParams(collective_id=0, has_side_effects=True, vmem_limit_bytes=32 << 20),
    )(thickness, velocity, packed, weights, *coefs, over, ids)

    def in_general():
        return general(thickness, velocity, *index, edge_weights, cell_area, edge_spacing, edge_length, coriolis)

    return lax.cond(mark[0, 0] > 0, in_general, lambda: (h, u))


def solution(mesh):
    return jax.shard_map(
        shards,
        mesh=mesh,
        in_specs=(
            P(None, "dom"),
            P(None, "dom"),
            P("dom", None),
            P("dom", None),
            P(None, "dom"),
            P(None, "dom"),
            P(None, "dom"),
            P(None, "dom"),
            P(None, "dom"),
            P("dom"),
            P("dom"),
            P("dom"),
            P("dom"),
        ),
        out_specs=(P(None, "dom"), P(None, "dom")),
        check_vma=False,
    )
```

```python
import functools

import jax
import jax.numpy as jnp
from jax import lax
from jax.experimental import pallas as pl
from jax.experimental.pallas import tpu as pltpu
from jax.sharding import PartitionSpec as P

gravity = 0.1
mixing = 0.2
time_step = 0.5
LANES = 128
TILES = 12
OFFSETS = (-2, -1, 1, 2)
VMEM = pltpu.VMEM
SMEM = pltpu.SMEM
TOP, LOW = slice(0, 8), slice(8, 16)


class Plan:
    rows = weights = ids = 0

    def __init__(self, terms, octets, first, chunks, cap, turns, weighted, apart):
        self.terms, self.octets, self.first, self.chunks = terms, octets, first, chunks
        self.cap, self.turns, self.weighted, self.apart = cap, turns, weighted, apart
        self.goals = 8 * terms if apart else 8
        self.row_at, self.weight_at, self.id_at = Plan.rows, Plan.weights, Plan.ids
        self.tiles, self.steps = cap // 8, cap // turns
        Plan.rows += octets * self.tiles
        Plan.weights += octets * self.tiles * weighted
        Plan.ids += octets * turns


AROUND = Plan(10, 6, 0, 48, 280, 5, True, False), Plan(10, 6, 48, 16, 104, 1, True, False)
PAIR = Plan(2, 6, 0, 16, 72, 1, False, True), Plan(2, 6, 16, 8, 40, 1, False, True)
SIDE = Plan(6, 2, 0, 48, 208, 2, True, False), Plan(6, 2, 48, 16, 80, 1, True, False)
SEND_E = Plan(1, 2, 0, 48, 112, 2, False, False)
SEND_C = Plan(1, 1, 0, 16, 64, 1, False, False)
ROWS, WEIGHTS, IDS = Plan.rows, Plan.weights, -(-Plan.ids // 8) * 8


def iota(axis):
    return lax.broadcasted_iota(jnp.int32, (8, LANES), axis)


def spread(row):
    return jnp.broadcast_to(row, (8, LANES))


def turn(x, shift):
    return pltpu.roll(x, shift, 0)


def lanes_at(position):
    return pl.ds(pl.multiple_of(position * LANES, LANES), LANES)


def sums_of_rows(parts, sub):
    for bit in (1, 2, 4):
        first = (sub & bit) == 0
        parts = [jnp.where(first, a, b) + turn(jnp.where(first, b, a), bit) for a, b in zip(parts[::2], parts[1::2])]
    return parts[0]


def build(plan, raw, scale, packed, weights, ids, over, chunks, keys, loads):
    sub, lane = iota(0), iota(1)
    tiles = -(-plan.chunks // 8)
    numbers = [sub + 8 * v for v in range(tiles)]

    def octet(o, carry):
        at = pl.ds(pl.multiple_of(o * 8, 8), 8)
        for k in range(plan.terms):
            chunks[k] = lax.shift_right_logical(raw[k, at, :], 7) - plan.first

        counts = [jnp.zeros((8, LANES), jnp.int32) for _ in range(tiles)]
        for k in range(plan.terms):
            parts = []
            for s in range(8):
                chunk = spread(chunks[k, s : s + 1, :])
                part = None
                for v in range(tiles):
                    hit = chunk == numbers[v]
                    seen = jnp.where(hit, counts[v], 0)
                    part = seen if part is None else part + seen
                    counts[v] = jnp.where(hit, counts[v] + 1, counts[v])
                parts.append(part)
            keys[k] = sums_of_rows(parts, sub)
        most = [spread(jnp.max(c, axis=1, keepdims=True)) for c in counts]
        upto = most
        for shift in (1, 2, 4):
            upto = [x + jnp.where(sub >= shift, turn(x, shift), 0) for x in upto]
        before = jnp.zeros((8, LANES), jnp.int32)
        starts = jnp.zeros((8, LANES), jnp.int32)
        for v in range(tiles):
            starts = starts + jnp.where(lane == numbers[v], upto[v] - most[v] + before, 0)
            before = before + spread(upto[v][7:8])
        for shift in (1, 2, 4):
            starts = starts + turn(starts, shift)
        over[...] = jnp.maximum(over[...], jnp.where(before > plan.cap, 1.0, 0.0))
        for k in range(plan.terms):
            chunk = chunks[k]
            inside = (chunk >= 0) & (chunk < plan.chunks)
            start = jnp.take_along_axis(starts, chunk & 127, axis=1, mode="promise_in_bounds")
            keys[k] = jnp.where(inside, start + keys[k], -1)
            loads[k] = (raw[k, at, :] & 127) | ((sub + 8 * k * plan.apart) << 7) | (jnp.where(inside, chunk, 0) << 12)
        places = [jnp.zeros((8, LANES), jnp.int32) for _ in range(plan.turns)]
        for top in range(0, plan.cap, 8 * TILES):
            tops = list(range(top, min(top + 8 * TILES, plan.cap), 8))
            size = len(tops)

            def match(k, found, tops=tops, size=size):
                load, weight = list(found[:size]), list(found[size:])
                for s in range(8):
                    wanted = spread(keys[k, s : s + 1, :])
                    value = spread(loads[k, s : s + 1, :])
                    if plan.weighted:
                        factor = spread(scale[k, pl.ds(o * 8 + s, 1), :])
                    for v in range(size):
                        here = wanted == sub + tops[v]
                        load[v] = jnp.where(here, value, load[v])
                        if plan.weighted:
                            weight[v] = jnp.where(here, factor, weight[v])
                return (*load, *weight)

            begin = [jnp.full((8, LANES), 16 << 7, jnp.int32)] * size
            begin += [jnp.zeros((8, LANES), jnp.float32)] * (size * plan.weighted)
            found = lax.fori_loop(0, plan.terms, match, tuple(begin))
            for v in range(size):
                load = found[v]
                offset = o * plan.tiles + tops[v] // 8
                packed[plan.row_at + offset] = load & 4095
                if plan.weighted:
                    weights[plan.weight_at + offset] = found[size + v]
                own = jnp.max(load >> 12, axis=1, keepdims=True)
                which, lane_at = divmod(tops[v], plan.steps)
                places[which] = places[which] + jnp.where(lane == sub + lane_at, own, 0)
        for i, place in enumerate(places):
            ids[pl.ds(plan.id_at + o * plan.turns + i, 1), :] = jnp.sum(place, axis=0, keepdims=True)
        return carry

    lax.fori_loop(0, plan.octets, octet, 0)


def plans_kernel(send_c, send_e, cell_edges, cell_orient, edge_cells, edge_edges, edge_weights, *rest):
    packed, weights, ids, over, around, factors, pair, side, signs, to_e, to_c, chunks, keys, loads = rest
    over[...] = jnp.zeros((8, LANES), jnp.float32)
    ids[...] = jnp.zeros((IDS, LANES), jnp.int32)
    for j in range(4):
        for q in range(4):
            to_e[0, 4 * j + q : 4 * j + q + 1, :] = send_e[j : j + 1, q * LANES : (q + 1) * LANES]
        for q in range(2):
            to_c[0, 2 * j + q : 2 * j + q + 1, :] = send_c[j : j + 1, q * LANES : (q + 1) * LANES]
    for g in range(48):
        at = slice(g * LANES, (g + 1) * LANES)
        for k in range(10):
            around[k, g : g + 1, :] = edge_edges[k : k + 1, at]
            factors[k, g : g + 1, :] = edge_weights[k : k + 1, at]
        for k in range(2):
            pair[k, g : g + 1, :] = edge_cells[k : k + 1, at]
    for g in range(16):
        at = slice(g * LANES, (g + 1) * LANES)
        for k in range(6):
            side[k, g : g + 1, :] = cell_edges[k : k + 1, at]
            signs[k, g : g + 1, :] = (2 * cell_orient[k : k + 1, at] - 1).astype(jnp.float32)
    tail = (packed, weights, ids, over, chunks, keys, loads)
    build(SEND_E, to_e, None, *tail)
    build(SEND_C, to_c, None, *tail)
    for i in range(2):
        build(AROUND[i], around, factors, *tail)
        build(PAIR[i], pair, None, *tail)
        build(SIDE[i], side, signs, *tail)


def gather(plan, lists, o, sources, sums):
    packed, weights, ids = lists

    def step(t, sums):
        sums = list(sums)
        turn_at = o * plan.turns + t
        tile_at = turn_at * (plan.steps // 8)
        for r in range(plan.steps):
            chunk = ids[plan.id_at + turn_at, r]
            load = spread(packed[plan.row_at + tile_at + r // 8, r % 8 : r % 8 + 1, :])
            pick, goal = load & 127, lax.shift_right_logical(load, 7)
            found = [jnp.take_along_axis(take(chunk), pick, axis=1, mode="promise_in_bounds") for take in sources]
            if plan.weighted:
                factor = spread(weights[plan.weight_at + tile_at + r // 8, r % 8 : r % 8 + 1, :])
                found = [value * factor for value in found]
            for d in range(plan.goals):
                mine = goal == d
                for i, value in enumerate(found):
                    j = d * len(sources) + i
                    sums[j] = jnp.where(mine, sums[j] + value if plan.weighted else value, sums[j])
        return tuple(sums)

    return lax.fori_loop(0, plan.turns, step, tuple(sums))


def zeros(count):
    return [jnp.zeros((8, LANES), jnp.float32) for _ in range(count)]


def both(*takes):
    return [functools.partial(take, rows) for take in takes for rows in (TOP, LOW)]


def table(ref):
    return lambda rows, chunk: ref[chunk, rows, :]


FIELDS = 3


def partner(me, b):
    return me + b - 2 * b * (me // b % 2)


def step_kernel(thickness, velocity, packed_in, weights_in, spacing_in, length_in, coriolis_in, area_in, over, ids, *rest):
    h_out, u_out, mark = rest[:3]
    (h0, u0, packed, weights, spacing, length, coriolis, area, loaded) = rest[3:12]
    (h, u, flux, tangent, cells, spread_sum, send_h, send_u, send_f, halo_h, halo_u, halo_f, near, sent, came) = rest[12:27]
    told, heard, told_sem, heard_sem = rest[27:]
    me = lax.axis_index("dom")
    count = lax.axis_size("dom")
    barrier = pltpu.get_barrier_semaphore()
    for offset in OFFSETS:
        peer = me + offset

        @pl.when((peer >= 0) & (peer < count))
        def _():
            pl.semaphore_signal(barrier, inc=1, device_id=(peer,), device_id_type=pl.DeviceIdType.MESH)

    rounds = count.bit_length() - 1
    for r in range(2, rounds):
        pl.semaphore_signal(barrier, inc=1, device_id=(partner(me, 2**r),), device_id_type=pl.DeviceIdType.MESH)
    mark[...] = over[...]

    def tell(r):
        return pltpu.make_async_remote_copy(
            src_ref=told.at[r],
            dst_ref=heard.at[r],
            send_sem=told_sem.at[r],
            recv_sem=heard_sem.at[r],
            device_id=(partner(me, lax.shift_left(1, r)),),
            device_id_type=pl.DeviceIdType.MESH,
        )

    def spread_mark(r):
        @pl.when((r >= 1) & (r <= rounds))
        def _():
            tell(r - 1).wait_recv()
            mark[...] = jnp.maximum(mark[...], heard[r - 1])

        @pl.when(r < rounds)
        def _():
            told[r] = mark[...]
            tell(r).start()

    lists = (packed, weights, ids)
    given = (thickness, velocity, packed_in, spacing_in, length_in, coriolis_in, area_in, weights_in)
    kept = (h0, u0, packed, spacing, length, coriolis, area, weights)
    copies = [pltpu.make_async_copy(a, b, loaded.at[i]) for i, (a, b) in enumerate(zip(given, kept))]
    for copy in copies:
        copy.start()
    sends, halos = (send_h, send_u, send_f), (halo_h, halo_u, halo_f)
    widths = (2, 4, 4)

    def copy_of(field, k, place, peer):
        at = pl.ds(place * widths[field], widths[field])
        return pltpu.make_async_remote_copy(
            src_ref=sends[field].at[k, at],
            dst_ref=halos[field].at[k, at],
            send_sem=sent.at[k, field, place],
            recv_sem=came.at[k, field, place],
            device_id=(peer,),
            device_id_type=pl.DeviceIdType.MESH,
        )

    def start(field, k):
        for place, offset in enumerate(OFFSETS):
            peer = me + offset

            @pl.when((peer >= 0) & (peer < count))
            def _():
                copy_of(field, k, place, peer).start()

    def arrive(field, k):
        for place, offset in enumerate(OFFSETS):
            origin = me - offset

            @pl.when((origin >= 0) & (origin < count))
            def _():
                copy_of(field, k, place, origin).wait_recv()

        near[: 4 * widths[field]] = halos[field][k]

    for place, offset in enumerate(OFFSETS):
        origin = me - offset

        @pl.when((origin < 0) | (origin >= count))
        def _():
            for halo, width in zip(halos, widths):
                for k in range(3):
                    halo[k, place * width : (place + 1) * width] = jnp.zeros((width, 16, LANES), jnp.float32)

    def send_edges(k, *refs):
        sources = both(*(table(source) for source, _ in refs))

        def octet(o, carry):
            found = gather(SEND_E, lists, o, sources, zeros(8 * len(sources)))
            for d in range(8):
                for i, (_, buffer) in enumerate(refs):
                    for j, rows in enumerate((TOP, LOW)):
                        buffer[k, o * 8 + d, rows, :] = found[d * len(sources) + 2 * i + j]
            return carry

        lax.fori_loop(0, 2, octet, 0)

    def send_cells(k, source):
        found = gather(SEND_C, lists, 0, both(table(source)), zeros(16))
        for d in range(8):
            for j, rows in enumerate((TOP, LOW)):
                send_h[k, d, rows, :] = found[2 * d + j]

    for i in range(3):
        copies[i].wait()
    for group in range(48):
        u[group] = u0[:, group * LANES : (group + 1) * LANES]
    for group in range(16):
        h[group] = h0[:, group * LANES : (group + 1) * LANES]
    send_edges(0, (u, send_u))
    send_cells(0, h)
    pl.semaphore_wait(barrier, jnp.minimum(me, 2) + jnp.minimum(count - 1 - me, 2) + max(rounds - 2, 0))
    start(0, 0)
    start(1, 0)
    for i in range(3, len(copies)):
        copies[i].wait()
    sub = iota(0)

    def running(x):
        for shift in (1, 2, 4):
            x = x + jnp.where(sub >= shift, turn(x, shift), 0.0)
        return x

    def sweep(plan, take, ref, fresh):
        def octet(o, carry):
            at = [o * 8 + d % 8 + d // 8 * 48 for d in range(plan.goals)]
            begin = zeros(2 * plan.goals) if fresh else [ref[a, rows, :] for a in at for rows in (TOP, LOW)]
            found = gather(plan, lists, o, both(take), begin)
            for d in range(plan.goals):
                for j, rows in enumerate((TOP, LOW)):
                    ref[at[d], rows, :] = found[2 * d + j]
            return carry

        lax.fori_loop(0, plan.octets, octet, 0)

    def edges_of(k, tau):
        def quad(q, carry):
            for e in range(4):
                group = q * 4 + e
                at = lanes_at(group)
                left, right = group, 48 + group
                step = [cells[right, rows, :] - cells[left, rows, :] for rows in (TOP, LOW)]
                mean = [0.5 * (cells[right, rows, :] + cells[left, rows, :]) for rows in (TOP, LOW)]
                column = [running(x) for x in step]
                column[1] = column[1] + spread(column[0][7:8])
                pressure = [gravity * (c - 0.5 * x) for c, x in zip(column, step)]
                now = [u[group, rows, :] for rows in (TOP, LOW)]
                upper = [
                    jnp.where(sub == 0, now[0], turn(now[0], 1)),
                    jnp.where(sub == 0, spread(now[0][7:8]), turn(now[1], 1)),
                ]
                lower = [
                    jnp.where(sub == 7, spread(now[1][0:1]), turn(now[0], 7)),
                    jnp.where(sub == 7, now[1], turn(now[1], 7)),
                ]
                gap, long, spin = [spread(ref[pl.ds(group, 1), :]) for ref in (spacing, length, coriolis)]
                for i, rows in enumerate((TOP, LOW)):
                    mix = mixing * (upper[i] + lower[i] - 2.0 * now[i])
                    fresh = u0[rows, at] + tau * (-pressure[i] / gap + spin * tangent[group, rows, :] + mix)
                    u[group, rows, :] = fresh
                    flux[group, rows, :] = fresh * mean[i] * long
            return carry

        lax.fori_loop(0, 12, quad, 0)

    def section(k, carry):
        tau = time_step / (3 - k).astype(jnp.float32)
        spread_mark(3 * k)
        sweep(AROUND[0], table(u), tangent, True)
        sweep(PAIR[0], table(h), cells, True)
        arrive(1, k)
        sweep(AROUND[1], table(near), tangent, False)
        arrive(0, k)
        sweep(PAIR[1], table(near), cells, False)
        spread_mark(3 * k + 1)
        edges_of(k, tau)

        later = jnp.minimum(k + 1, 2)

        @pl.when(k < 2)
        def _():
            send_edges_pair(k, later)
            start(2, k)
            start(1, later)

        @pl.when(k == 2)
        def _():
            send_edges(2, (flux, send_f))
            start(2, 2)

        sweep(SIDE[0], table(flux), spread_sum, True)
        spread_mark(3 * k + 2)
        arrive(2, k)
        sweep(SIDE[1], table(near), spread_sum, False)
        for group in range(16):
            at = slice(group * LANES, (group + 1) * LANES)
            own = spread(area[group : group + 1, :])
            for rows in (TOP, LOW):
                h[group, rows, :] = h0[rows, at] - tau * spread_sum[group, rows, :] / own

        @pl.when(k < 2)
        def _():
            send_cells(later, h)
            start(0, later)

        return carry

    def send_edges_pair(k, later):
        sources = both(table(flux), table(u))

        def octet(o, carry):
            found = gather(SEND_E, lists, o, sources, zeros(32))
            for d in range(8):
                at = o * 8 + d
                for j, rows in enumerate((TOP, LOW)):
                    send_f[k, at, rows, :] = found[4 * d + j]
                    send_u[later, at, rows, :] = found[4 * d + 2 + j]
            return carry

        lax.fori_loop(0, 2, octet, 0)

    lax.fori_loop(0, 3, section, 0)
    for group in range(48):
        u_out[:, group * LANES : (group + 1) * LANES] = u[group]
    for group in range(16):
        h_out[:, group * LANES : (group + 1) * LANES] = h[group]
    for r in range(rounds):
        tell(r).wait_send()
    for field in range(FIELDS):
        for k in range(3):
            for place, offset in enumerate(OFFSETS):
                peer = me + offset

                @pl.when((peer >= 0) & (peer < count))
                def _():
                    copy_of(field, k, place, peer).wait_send()


def floats(*shape):
    return jax.ShapeDtypeStruct(shape, jnp.float32)


def ints(*shape):
    return jax.ShapeDtypeStruct(shape, jnp.int32)


def whole(count):
    return [pl.BlockSpec(memory_space=VMEM)] * count


def held(dtype, *shapes):
    return [VMEM(shape, dtype) for shape in shapes]


def shifted(block, axis, distance):
    devices = range(lax.axis_size(axis))
    route = [(i - distance, i) for i in devices if i - distance in devices]
    return lax.ppermute(block, axis, route)


def peer_offsets(slot_count):
    half = slot_count // 2
    return [place - half if place < half else place - half + 1 for place in range(slot_count)]


def state_halo(cell_blocks, edge_blocks):
    slot_count = cell_blocks.shape[0]
    offsets = peer_offsets(slot_count)
    arrived = {}
    for place, offset in enumerate(offsets):
        arrived[offset] = shifted((cell_blocks[place], edge_blocks[place]), "dom", offset)
    cell_parts = [arrived[offset][0] for offset in offsets]
    edge_parts = [arrived[offset][1] for offset in offsets]
    return (jnp.concatenate(cell_parts, axis=0), jnp.concatenate(edge_parts, axis=0))


def flux_halo(flux_blocks):
    slot_count = flux_blocks.shape[0]
    offsets = peer_offsets(slot_count)
    arrived = {}
    for place, offset in enumerate(offsets):
        arrived[offset] = shifted(flux_blocks[place], "dom", offset)
    return jnp.concatenate([arrived[offset] for offset in offsets], axis=0)


def general(
    thickness,
    velocity,
    send_cells,
    send_edges,
    cell_edges,
    cell_orient,
    edge_cells,
    edge_edges,
    edge_weights,
    cell_area,
    edge_spacing,
    edge_length,
    coriolis,
):
    levels = thickness.shape[0]
    edge_count = velocity.shape[1]
    cell_count = thickness.shape[1]
    signs = (2 * cell_orient - 1).astype(jnp.float32).T
    pair_index = edge_cells.reshape(-1)
    around_index = edge_edges.reshape(-1)
    side_index = cell_edges.T.reshape(-1)
    rows_h0 = thickness.T
    rows_u0 = velocity.T
    rows_h = rows_h0
    rows_u = rows_u0
    for section in range(3):
        step_size = time_step / (3 - section)
        cell_blocks = jnp.take(rows_h, send_cells, axis=0)
        edge_blocks = jnp.take(rows_u, send_edges, axis=0)
        halo_h, halo_u = state_halo(cell_blocks, edge_blocks)
        ext_h = jnp.concatenate([rows_h, halo_h], axis=0)
        ext_u = jnp.concatenate([rows_u, halo_u], axis=0)
        ext_p = gravity * (jnp.cumsum(ext_h, axis=1) - 0.5 * ext_h)
        table = jnp.concatenate([ext_h, ext_p], axis=1)
        picked = jnp.take(table, pair_index, axis=0).reshape(2, edge_count, 2 * levels)
        left_h = picked[0, :, :levels]
        right_h = picked[1, :, :levels]
        gradient = (picked[1, :, levels:] - picked[0, :, levels:]) / edge_spacing[:, None]
        beside_all = jnp.take(ext_u, around_index, axis=0).reshape(-1, edge_count, levels)
        tangent = jnp.sum(beside_all * edge_weights[:, :, None], axis=0)
        upper = jnp.concatenate([rows_u[:, :1], rows_u[:, :-1]], axis=1)
        lower = jnp.concatenate([rows_u[:, 1:], rows_u[:, -1:]], axis=1)
        blend = mixing * (upper + lower - 2.0 * rows_u)
        u_next = rows_u0 + step_size * (-gradient + coriolis[:, None] * tangent + blend)
        flux = u_next * 0.5 * (left_h + right_h) * edge_length[:, None]
        halo_f = flux_halo(jnp.take(flux, send_edges, axis=0))
        ext_f = jnp.concatenate([flux, halo_f], axis=0)
        sides = jnp.take(ext_f, side_index, axis=0).reshape(cell_count, -1, levels)
        spread = jnp.sum(sides * signs[:, :, None], axis=1)
        rows_h = rows_h0 - step_size * spread / cell_area[:, None]
        rows_u = u_next
    return (rows_h.T, rows_u.T)


def shards(
    thickness,
    velocity,
    send_cells,
    send_edges,
    cell_edges,
    cell_orient,
    edge_cells,
    edge_edges,
    edge_weights,
    cell_area,
    edge_spacing,
    edge_length,
    coriolis,
):
    index = (send_cells, send_edges, cell_edges, cell_orient, edge_cells, edge_edges)
    around, side = (10, 48, LANES), (6, 16, LANES)
    packed, weights, ids, over = pl.pallas_call(
        plans_kernel,
        name="plan_gathers",
        in_specs=whole(7),
        out_shape=[ints(ROWS, 8, LANES), floats(WEIGHTS, 8, LANES), ints(IDS, LANES), floats(8, LANES)],
        out_specs=whole(4),
        scratch_shapes=held(jnp.int32, around)
        + held(jnp.float32, around)
        + held(jnp.int32, (2, 48, LANES), side)
        + held(jnp.float32, side)
        + held(jnp.int32, (1, 16, LANES), (1, 8, LANES), *[(10, 8, LANES)] * 3),
        compiler_params=pltpu.CompilerParams(vmem_limit_bytes=24 << 20),
    )(*index, edge_weights)
    coefs = [x.reshape(48, LANES) for x in (edge_spacing, edge_length, coriolis)] + [cell_area.reshape(16, LANES)]
    rows, groups, halo = (48, LANES), (48, 16, LANES), (3, 16, 16, LANES)
    h, u, mark = pl.pallas_call(
        step_kernel,
        name="three_sections",
        in_specs=[pl.BlockSpec(memory_space=pl.ANY)] * 8 + whole(1) + [pl.BlockSpec(memory_space=SMEM)],
        out_shape=[floats(16, 16 * LANES), floats(16, 48 * LANES), floats(8, LANES)],
        out_specs=whole(3),
        scratch_shapes=held(jnp.float32, (16, 16 * LANES), (16, 48 * LANES))
        + held(jnp.int32, (ROWS, 8, LANES))
        + held(jnp.float32, (WEIGHTS, 8, LANES), rows, rows, rows, (16, LANES))
        + [pltpu.SemaphoreType.DMA((8,))]
        + held(jnp.float32, (16, 16, LANES), groups, groups, groups, (96, 16, LANES), (16, 16, LANES))
        + held(jnp.float32, (3, 8, 16, LANES), halo, halo, (3, 8, 16, LANES), halo, halo, (16, 16, LANES))
        + [pltpu.SemaphoreType.DMA((3, FIELDS, 4)), pltpu.SemaphoreType.DMA((3, FIELDS, 4))]
        + held(jnp.float32, (7, 8, LANES), (7, 8, LANES))
        + [pltpu.SemaphoreType.DMA((7,)), pltpu.SemaphoreType.DMA((7,))],
        compiler_params=pltpu.CompilerParams(collective_id=0, has_side_effects=True, vmem_limit_bytes=32 << 20),
    )(thickness, velocity, packed, weights, *coefs, over, ids)

    def in_general():
        return general(thickness, velocity, *index, edge_weights, cell_area, edge_spacing, edge_length, coriolis)

    return lax.cond(mark[0, 0] > 0, in_general, lambda: (h, u))


def solution(mesh):
    return jax.shard_map(
        shards,
        mesh=mesh,
        in_specs=(
            P(None, "dom"),
            P(None, "dom"),
            P("dom", None),
            P("dom", None),
            P(None, "dom"),
            P(None, "dom"),
            P(None, "dom"),
            P(None, "dom"),
            P(None, "dom"),
            P("dom"),
            P("dom"),
            P("dom"),
            P("dom"),
        ),
        out_specs=(P(None, "dom"), P(None, "dom")),
        check_vma=False,
    )
```
